512 devices in a mesh: dp: 64 (over z_lo, y, x), emb: 8 (over z_hi, core).
Axes of the slice: x: 4, y: 8, z: 8 (z_hi: 4, z_lo: 2; z = z_hi * 2 + z_lo), core: 2. Of those that a mesh axis runs over, the one named last changes fastest.
Arguments:
- image_emb: bfloat16 [1152, 16384], P('emb', 'dp'), may hold values from -6 to 6
- text_feat: bfloat16 [1152, 16384], P(None, 'dp'), may hold values from -6 to 6
- head_weight: bfloat16 [1152, 1152], P('emb'), may hold values from -0.1875 to 0.1875
- logit_scale: float32 [1], replicated, may hold values from 4 to 16
- logit_bias: float32 [1], replicated, may hold values from -3 to -1
Outputs:
- image_grad: bfloat16 [1152, 16384], P('emb', 'dp')
- head_grad: float32 [1152, 1152], P('emb')
The draws below stay inside these ranges and needn't reach their ends.
All inputs are finite; a program needn't handle non-finite values.
Results may differ from the reference program's by a relative error of at most 0.022.
Values may be sent and summed in bfloat16 or wider, within the bound.
A program may use at most 64 MiB of HBM per device.

```python
import math
import jax
import jax.numpy as jnp
from jax import lax

D = 1152
TOK_DEV = 256
REACH = 6
TOKENS = 16384
N_DP = 64
N_EMB = 8


def shard_levels(rng, extent, cuts, low, top_value):
    factor_of = 1.0
    for position, parts in cuts:
        steps = jax.random.uniform(jax.random.fold_in(jax.random.fold_in(rng, 6), position), (parts,), jnp.float32, low / len(cuts), top_value / len(cuts))
        factor_of = factor_of * jnp.repeat(jnp.exp(steps), extent[position] // parts).reshape((-1,) + (1,) * (len(extent) - 1 - position))
    return factor_of


def bell_draw(stream_key, dims, deviation, limit, cuts=(), held_as=jnp.bfloat16):
    result = jax.random.normal(stream_key, dims, jnp.float32) * deviation
    if len(cuts) > 0:
        result = shard_levels(stream_key, dims, cuts, -0.22, 0.18) * result
    return jnp.clip(result, min=-limit, max=limit).astype(held_as)


def setup_inputs(seed: int = 0) -> dict:
    splits = jax.random.split(jax.random.key(seed), 6)
    return {
        "image_emb": bell_draw(splits[0], (D, TOKENS), 1.0, 6.0, ((0, 8), (1, 64))),
        "text_feat": bell_draw(splits[1], (D, TOKENS), 1.0, 6.0, ((1, 64),)),
        "head_weight": bell_draw(splits[2], (D, D), D ** -0.5, 0.1875, ((0, 8),)),
        "logit_scale": jnp.clip(jnp.exp(jax.random.uniform(splits[3], (1,), jnp.float32, math.log(4.0), math.log(16.0))), 4.0, 16.0),
        "logit_bias": jnp.clip(jax.random.uniform(splits[4], (1,), jnp.float32, -3.0, -1.0), -3.0, -1.0),
    }


EPSILON = 1e-06

def reference(image_emb, text_feat, head_weight, logit_scale, logit_bias):
    local = image_emb.astype(jnp.float32)
    text_raw = jnp.dot(head_weight, text_feat, preferred_element_type=jnp.float32)
    image_len = jnp.sqrt(lax.optimization_barrier(jnp.sum(local * local, 0)) + EPSILON)
    text_len = jnp.sqrt(lax.optimization_barrier(jnp.sum(text_raw * text_raw, 0)) + EPSILON)
    image_unit = (local / image_len).astype(jnp.bfloat16)
    text_unit = (text_raw / text_len).astype(jnp.bfloat16)
    scale = logit_scale[0]
    offset = logit_bias[0]
    group = D // N_EMB
    image_blocks = image_unit.reshape(D, N_DP, TOK_DEV).transpose(1, 0, 2)
    text_blocks = text_unit.reshape(D, N_DP, TOK_DEV).transpose(1, 0, 2)
    image_split = image_blocks.astype(jnp.float32).reshape(N_DP, N_EMB, group, TOK_DEV)
    positions = jnp.arange(TOK_DEV, dtype=jnp.int32)
    same = positions[:, None] == positions[None, :]
    image_acc = jnp.zeros((N_DP, D, TOK_DEV), jnp.float32)
    text_acc = jnp.zeros((N_DP, D, TOK_DEV), jnp.float32)
    for shift_by in range(-REACH, REACH + 1):
        rolled = jnp.roll(text_blocks, -shift_by, axis=0)
        rolled_split = rolled.astype(jnp.float32).reshape(N_DP, N_EMB, group, TOK_DEV)
        partial_value = jnp.einsum('nkei,nkej->nkij', image_split, rolled_split)
        rounded = lax.optimization_barrier(partial_value.astype(jnp.bfloat16)).astype(jnp.float32)
        cosine = lax.optimization_barrier(jnp.sum(rounded, 1))
        logits = scale * cosine + offset
        if shift_by == 0:
            sign = jnp.where(same, jnp.float32(1.0), jnp.float32(-1.0))
        else:
            sign = jnp.full((TOK_DEV, TOK_DEV), -1.0, jnp.float32)
        weights = (-scale * sign * jax.nn.sigmoid(-sign * logits)).astype(jnp.bfloat16).astype(jnp.float32)
        image_part = jnp.einsum('nej,nij->nei', rolled.astype(jnp.float32), weights)
        text_part = jnp.einsum('nei,nij->nej', image_blocks.astype(jnp.float32), weights)
        image_acc = image_acc + image_part
        text_acc = text_acc + jnp.roll(text_part, shift_by, axis=0)
    image_dir = image_acc.transpose(1, 0, 2).reshape(D, TOKENS)
    text_dir = text_acc.transpose(1, 0, 2).reshape(D, TOKENS)
    image_f = image_unit.astype(jnp.float32)
    text_f = text_unit.astype(jnp.float32)
    image_proj = lax.optimization_barrier(jnp.sum(image_f * image_dir, 0))
    text_proj = lax.optimization_barrier(jnp.sum(text_f * text_dir, 0))
    image_grad = ((image_dir - image_f * image_proj) / image_len).astype(jnp.bfloat16)
    text_grad = ((text_dir - text_f * text_proj) / text_len).astype(jnp.bfloat16)
    head_grad = jnp.dot(text_grad, text_feat.T, preferred_element_type=jnp.float32)
    return (image_grad, head_grad)
```

```python
import functools

import jax
import jax.numpy as jnp
from jax import lax
from jax.experimental import pallas as pl
from jax.experimental.pallas import tpu as pltpu
from jax.sharding import PartitionSpec as P

REACH = 6
EPSILON = 1e-06
N_ZLO, N_Y, N_X = 2, 8, 4
LANES = 128
ORDER = (0, 1, -1, 4, -4, 3, -3, 2, -2, 5, -5, 6, -6)
SLOT = {o: i for i, o in enumerate(ORDER)}
NEAR, MIDDLE = 7, 11
MESH = pl.DeviceIdType.MESH
BF16, F32 = jnp.bfloat16, jnp.float32


def up(value, step):
    return -(-value // step) * step


def kernel(
    sizes,
    image_hbm,
    feat_hbm,
    weight_hbm,
    scale_ref,
    bias_ref,
    image_out,
    head_out,
    image_ref,
    feat_ref,
    weight_ref,
    turn_f,
    swap_src,
    swap_dst,
    images,
    text_nat,
    text,
    weights,
    grad,
    text_part,
    pair_dst,
    line_src,
    line_dst,
    mid_dst,
    dirs,
    dirs_back,
    back_src,
    back_dst,
    head_src,
    head_dst,
    col_src,
    col_dst,
    col_sum,
    head_sum,
    load,
    swap_s,
    swap_r,
    win_s,
    win_r,
    gat_s,
    gat_r,
    fwd_s,
    fwd_r,
    pair_s,
    pair_r,
    line_s,
    line_r,
    mid_s,
    mid_r,
    ret_s,
    ret_r,
    back_s,
    back_r,
    head_s,
    head_r,
    col_s,
    col_r,
    cga_s,
    cga_r,
    hga_s,
    hga_r,
):
    n_dp, n_emb, depth, pairs, width, chunk, piece = sizes
    tail = depth - LANES
    rows = pairs // n_emb
    n_hi = n_emb // 2
    n_group, n_col = N_ZLO * N_X, N_Y
    wide = LANES * n_emb + LANES
    slots = 2 * REACH + 1
    me = lax.axis_index("dp")
    k = lax.axis_index("emb")
    hi, core = k // 2, k % 2
    x_at, y_at, z_at = me % N_X, (me // N_X) % N_Y, me // (N_X * N_Y)
    first_group = (z_at * N_X + x_at) * (1 - core) + y_at * core
    second_group = y_at * (1 - core) + (z_at * N_X + x_at) * core

    def emb_peer(m):
        return (me, (k + m) % n_emb)

    def dp_peer(offset):
        return ((me + offset + n_dp) % n_dp, k)

    partner = (me, k + 1 - 2 * core)

    def hi_of(m):
        return (hi + m) % n_hi

    def line_peer(m):
        return (me, 2 * hi_of(m) + core)

    def chip_at(plane, line):
        return (plane // N_X) * (N_X * N_Y) + line * N_X + plane % N_X

    def group_of(m):
        return (first_group + m) % n_group

    def group_peer(m):
        to = group_of(m)
        here, there = chip_at(to, y_at), chip_at(z_at * N_X + x_at, to)
        return (here * (1 - core) + there * core, k)

    def col_of(m):
        return (second_group + m) % n_col

    def col_peer(m):
        to = col_of(m)
        here, there = chip_at(z_at * N_X + x_at, to), chip_at(to, y_at)
        return (here * (1 - core) + there * core, k)

    def at16(start, size):
        return pl.ds(pl.multiple_of(start, 16), size)

    def push(src, dst, send, recv, peer):
        copy = pltpu.make_async_remote_copy(
            src_ref=src,
            dst_ref=dst,
            send_sem=send,
            recv_sem=recv,
            device_id=peer,
            device_id_type=MESH,
        )
        copy.start()
        return copy

    def slot(o):
        return pl.ds(rows * SLOT[o], rows)

    def loaded(i, src, dst):
        copy = pltpu.make_async_copy(src, dst, load.at[i])
        copy.start()
        return copy

    loads = [
        loaded(0, image_hbm, image_ref),
        loaded(1, weight_hbm, weight_ref),
        loaded(2, feat_hbm, feat_ref),
    ]

    greeted = (
        [emb_peer(m) for m in (4, 3, 5, 2, 6, 1, 7)]
        + [dp_peer(o) for o in (1, -1, N_X, -N_X, N_X - 1, 1 - N_X, N_X + 1, -N_X - 1)]
        + [group_peer(m) for m in range(1, n_group)]
        + [col_peer(m) for m in range(1, n_col)]
    )
    barrier = pltpu.get_barrier_semaphore()
    for peer in greeted:
        pl.semaphore_signal(barrier, inc=1, device_id=peer, device_id_type=MESH)

    turn_f[LANES:, :] = jnp.zeros((LANES, pairs), F32)
    loads[0].wait()
    turn_f[:LANES, :] = image_ref[:LANES, :].astype(F32)
    turn_f[pl.ds(pl.multiple_of(LANES + tail * k, 16), tail), :] = image_ref[LANES:, :].astype(F32)
    swap_src[...] = jnp.transpose(turn_f[...]).astype(BF16)
    swap_dst[pl.ds(k, 1)] = swap_src[at16(rows * k, rows), :][None]
    pl.semaphore_wait(barrier, len(greeted))

    swaps = [
        push(
            swap_src.at[at16(rows * ((k + m) % n_emb), rows), :],
            swap_dst.at[k],
            swap_s.at[m],
            swap_r.at[m],
            emb_peer(m),
        )
        for m in range(1, n_emb)
    ]
    own_text = at16(depth * k, depth)
    loads[1].wait()
    loads[2].wait()
    text_nat[own_text, :] = jnp.dot(
        weight_ref[...], feat_ref[...], preferred_element_type=F32
    ).astype(BF16)

    upper, lower = line_peer(1), line_peer(n_hi - 1)
    cut = up(depth // 2, 16)
    gathers = [
        push(text_nat.at[own_text, :], text_nat.at[own_text, :], gat_s.at[0], gat_r.at[0], upper),
        push(text_nat.at[own_text, :], text_nat.at[own_text, :], gat_s.at[1], gat_r.at[1], lower),
    ]
    forwards = [
        push(text_nat.at[own_text, :], text_nat.at[own_text, :], fwd_s.at[0], fwd_r.at[0], partner)
    ]

    for copy in swaps:
        copy.wait_recv()
    raw = [swap_dst[j, :, :LANES].astype(F32) for j in range(n_emb)]
    raw.append(sum(swap_dst[j, :, LANES:].astype(F32) for j in range(n_emb)))
    square = sum(jnp.sum(r * r, axis=1, keepdims=True) for r in raw)
    image_inv = 1.0 / jnp.sqrt(square + EPSILON)
    home = slot(0)
    for j, r in enumerate(raw):
        images[home, LANES * j : LANES * (j + 1)] = (r * image_inv).astype(BF16)
    window = {}

    def pass_on(have, o):
        window[o] = push(
            images.at[slot(have), :],
            images.at[slot(o), :],
            win_s.at[SLOT[o]],
            win_r.at[SLOT[o]],
            dp_peer(have - o),
        )

    for o in (1, -1, N_X, -N_X, N_X - 1, 1 - N_X):
        pass_on(0, o)

    below = at16(depth * (2 * ((hi + n_hi - 1) % n_hi) + core), depth)
    above = at16(depth * (2 * ((hi + 1) % n_hi) + core), depth)
    across = depth * (2 * ((hi + 2) % n_hi) + core)
    below_cut = at16(depth * (2 * ((hi + n_hi - 1) % n_hi) + core), cut)
    above_cut = at16(depth * (2 * ((hi + 1) % n_hi) + core) + cut, depth - cut)
    gathers[0].wait_recv()
    gathers.append(
        push(text_nat.at[below_cut, :], text_nat.at[below_cut, :], gat_s.at[2], gat_r.at[2], upper)
    )
    gathers[1].wait_recv()
    gathers.append(
        push(text_nat.at[above_cut, :], text_nat.at[above_cut, :], gat_s.at[3], gat_r.at[3], lower)
    )
    for i, come in ((1, below), (2, above)):
        forwards.append(
            push(text_nat.at[come, :], text_nat.at[come, :], fwd_s.at[i], fwd_r.at[i], partner)
        )

    for near in (1, -1):
        window[near].wait_recv()
        for o in (N_X + 2, N_X + 1, 2):
            pass_on(near, near * o)

    gathers[2].wait_recv()
    gathers[3].wait_recv()
    come = at16(across, depth)
    forwards.append(
        push(text_nat.at[come, :], text_nat.at[come, :], fwd_s.at[3], fwd_r.at[3], partner)
    )

    for copy in forwards:
        copy.wait_recv()
    if LANES > tail * n_emb:
        text[LANES * n_emb + tail * n_emb :, :] = jnp.zeros((LANES - tail * n_emb, pairs), BF16)
    square = jnp.zeros((1, pairs), F32)
    for j in range(n_emb):
        part = text_nat[depth * j : depth * (j + 1), :]
        text[LANES * j : LANES * (j + 1), :] = part[:LANES]
        text[LANES * n_emb + tail * j : LANES * n_emb + tail * (j + 1), :] = part[LANES:]
        wide_part = part.astype(F32)
        square = square + jnp.sum(wide_part * wide_part, axis=0, keepdims=True)
    text_inv = 1.0 / jnp.sqrt(square + EPSILON)

    scale, bias = scale_ref[0], bias_ref[0]

    def meet(first, last):
        at = pl.ds(rows * first, rows * (last - first))
        cosine = jnp.dot(images[at, :], text[...], preferred_element_type=F32) * text_inv
        logits = scale * cosine + bias
        if first == 0:
            row_ids = lax.broadcasted_iota(jnp.int32, logits.shape, 0)
            col_ids = lax.broadcasted_iota(jnp.int32, logits.shape, 1)
            same = (row_ids < rows) & (col_ids - rows * k == row_ids)
            sign = jnp.where(same, jnp.float32(1.0), jnp.float32(-1.0))
        else:
            sign = jnp.float32(-1.0)
        sig = 1.0 / (1.0 + jnp.exp(sign * logits))
        value = (-scale * sign * sig * text_inv).astype(BF16)
        weights[at, :] = value
        return jnp.sum(value.astype(F32) * cosine, axis=0, keepdims=True)

    def turn_back(first, last):
        at = pl.ds(rows * first, rows * (last - first))
        dirs[at, :] = lax.dot_general(
            weights[at, :], text[...], (((1,), (1,)), ((), ())), preferred_element_type=F32
        ).astype(BF16)

    def text_side(first, last):
        at = pl.ds(rows * first, rows * (last - first))
        return lax.dot_general(
            images[at, :], weights[at, :], (((0,), (0,)), ((), ())), preferred_element_type=F32
        )

    for o in ORDER[3:NEAR]:
        window[o].wait_recv()
    inner = meet(0, NEAR)
    for o in ORDER[NEAR:MIDDLE]:
        window[o].wait_recv()
    inner = inner + meet(NEAR, MIDDLE)
    grad[...] = text_side(0, MIDDLE)
    for o in ORDER[MIDDLE:]:
        window[o].wait_recv()
    inner = (inner + meet(MIDDLE, len(ORDER))) * text_inv

    late = text_side(MIDDLE, len(ORDER))
    for j in range(n_emb):
        for at, size, to in ((LANES * j, LANES, 0), (LANES * n_emb + tail * j, tail, LANES)):
            part = grad[at : at + size, :] + late[at : at + size]
            part = part - text[at : at + size, :].astype(F32) * inner
            text_part[depth * j + to : depth * j + to + size, :] = part.astype(BF16)
    paired = {}
    for m in (2, 1, 3, 0):
        theirs = at16(depth * (2 * hi_of(m) + 1 - core), depth)
        paired[m] = push(text_part.at[theirs, :], pair_dst.at[m], pair_s.at[m], pair_r.at[m], partner)

    turn_back(0, len(ORDER))
    returns = {}

    def give_back(o, step):
        returns[o] = push(
            dirs.at[slot(o), :],
            dirs_back.at[slot(o), :],
            ret_s.at[SLOT[o]],
            ret_r.at[SLOT[o]],
            dp_peer(step),
        )

    def collect(o, sources):
        value = dirs[slot(o), :].astype(F32)
        for source in sources:
            returns[source].wait_recv()
            value = value + dirs_back[slot(source), :].astype(F32)
        return value

    def summed(m):
        paired[m].wait_recv()
        mine = at16(depth * (2 * hi_of(m) + core), depth)
        return text_part[mine, :].astype(F32) + pair_dst[m].astype(F32)

    first, second = pl.ds(0, cut), pl.ds(cut, depth - cut)
    line_src[0] = summed(2).astype(BF16)
    lines = [
        push(line_src.at[0, first, :], mid_dst.at[first, :], mid_s.at[0], mid_r.at[0], upper),
        push(line_src.at[0, second, :], mid_dst.at[second, :], mid_s.at[1], mid_r.at[1], lower),
    ]
    rising, falling = summed(1), summed(3)
    line_src[1, cut:, :] = rising[cut:].astype(BF16)
    line_src[2, :cut, :] = falling[:cut].astype(BF16)

    def line(i, j, part, peer):
        return push(line_src.at[i, part, :], line_dst.at[i, part, :], line_s.at[j], line_r.at[j], peer)

    lines.append(line(1, 0, second, upper))
    lines.append(line(2, 1, first, lower))
    lines[0].wait_recv()
    line_src[1, :cut, :] = (rising[:cut] + mid_dst[:cut, :].astype(F32)).astype(BF16)
    lines.append(line(1, 2, first, upper))
    lines[1].wait_recv()
    line_src[2, cut:, :] = (falling[cut:] + mid_dst[cut:, :].astype(F32)).astype(BF16)
    lines.append(line(2, 3, second, lower))
    for way in (1, -1):
        give_back(5 * way, N_X * way)
        give_back(3 * way, (N_X - 1) * way)
        give_back(6 * way, (N_X + 1) * way)
        give_back(2 * way, way)
        give_back(4 * way, N_X * way)
    for copy in swaps + gathers + forwards + list(window.values()):
        copy.wait_send()
    total = summed(0)
    for copy in lines[2:]:
        copy.wait_recv()
    total = total + line_dst[1].astype(F32) + line_dst[2].astype(F32)

    share = lax.dot_general(
        total.astype(BF16), feat_ref[...], (((1,), (1,)), ((), ())), preferred_element_type=F32
    )
    tiles = width // LANES
    for c in range(tiles):
        head_src[depth * c : depth * (c + 1), :] = share[:, LANES * c : LANES * (c + 1)].astype(BF16)
    if chunk * n_group > depth * tiles:
        head_src[depth * tiles :, :] = jnp.zeros((chunk * n_group - depth * tiles, LANES), BF16)
    heads = [
        push(
            head_src.at[at16(chunk * group_of(m), chunk), :],
            head_dst.at[m],
            head_s.at[m],
            head_r.at[m],
            group_peer(m),
        )
        for m in range(1, n_group)
    ]

    for way in (1, -1):
        dirs[slot(way), :] = collect(way, (2 * way, 5 * way, 6 * way)).astype(BF16)
        give_back(way, way)

    total = head_src[at16(chunk * first_group, chunk), :].astype(F32)
    for m in range(1, n_group):
        heads[m - 1].wait_recv()
        total = total + head_dst[m].astype(F32)
    col_src[:chunk, :] = total.astype(BF16)
    if piece * n_col > chunk:
        col_src[chunk:, :] = jnp.zeros((piece * n_col - chunk, LANES), BF16)
    cols = [
        push(col_src.at[at16(piece * col_of(m), piece), :], col_dst.at[m], col_s.at[m], col_r.at[m], col_peer(m))
        for m in range(1, n_col)
    ]

    for copy in lines + list(paired.values()) + heads:
        copy.wait_send()
    way = collect(0, (1, -1, 3, -3, 4, -4))
    unit = images[home, :].astype(F32)
    along = jnp.sum(unit * way, axis=1, keepdims=True)
    image_grad = ((way - unit * along) * image_inv).astype(BF16)
    for j in range(n_emb):
        back_src[j, :, :LANES] = image_grad[:, LANES * j : LANES * (j + 1)]
        back_src[j, :, LANES:] = image_grad[:, LANES * n_emb :]
    own_rows = at16(rows * k, rows)
    backs = [
        push(back_src.at[(k + m) % n_emb], back_dst.at[own_rows, :], back_s.at[m], back_r.at[m], emb_peer(m))
        for m in range(1, n_emb)
    ]
    back_dst[own_rows, :] = back_src[pl.ds(k, 1)][0]

    own_piece = at16(piece * second_group, piece)
    total = col_src[own_piece, :].astype(F32)
    for m in range(1, n_col):
        cols[m - 1].wait_recv()
        total = total + col_dst[m].astype(F32)
    col_sum[own_piece, :] = total.astype(BF16)
    col_gathers = [
        push(col_sum.at[own_piece, :], col_sum.at[own_piece, :], cga_s.at[m], cga_r.at[m], col_peer(m))
        for m in range(1, n_col)
    ]
    for copy in col_gathers:
        copy.wait_recv()
    own_chunk = at16(chunk * first_group, chunk)
    head_sum[own_chunk, :] = col_sum[:chunk, :]
    head_gathers = [
        push(col_sum.at[pl.ds(0, chunk), :], head_sum.at[own_chunk, :], hga_s.at[m], hga_r.at[m], group_peer(m))
        for m in range(1, n_group)
    ]

    for copy in backs:
        copy.wait_recv()
    turn_f[...] = jnp.transpose(back_dst[...].astype(F32))
    image_out[:LANES, :] = turn_f[:LANES, :].astype(BF16)
    image_out[LANES:, :] = turn_f[pl.ds(pl.multiple_of(LANES + tail * k, 16), tail), :].astype(BF16)

    for copy in list(returns.values()) + backs + cols + col_gathers:
        copy.wait_send()
    for copy in head_gathers:
        copy.wait_recv()
    for c in range(tiles):
        head_out[:, LANES * c : LANES * (c + 1)] = head_sum[depth * c : depth * (c + 1), :]

    for copy in head_gathers:
        copy.wait_send()


def on_device(image_emb, text_feat, head_weight, logit_scale, logit_bias):
    n_dp, n_emb = lax.axis_size("dp"), lax.axis_size("emb")
    depth, pairs = image_emb.shape
    width = text_feat.shape[0]
    rows = pairs // n_emb
    n_hi = n_emb // 2
    n_group, n_col = N_ZLO * N_X, N_Y
    slots = 2 * REACH + 1
    wide = LANES * n_emb + LANES
    chunk = up(depth * (width // LANES), 16 * n_group) // n_group
    piece = up(chunk, 16 * n_col) // n_col
    sizes = (n_dp, n_emb, depth, pairs, width, chunk, piece)
    scratch = [
        pltpu.VMEM((depth, pairs), BF16),
        pltpu.VMEM((width, pairs), BF16),
        pltpu.VMEM((depth, width), BF16),
        pltpu.VMEM((2 * LANES, pairs), F32),
        pltpu.VMEM((pairs, 2 * LANES), BF16),
        pltpu.VMEM((n_emb, rows, 2 * LANES), BF16),
        pltpu.VMEM((rows * slots, wide), BF16),
        pltpu.VMEM((depth * n_emb, pairs), BF16),
        pltpu.VMEM((wide, pairs), BF16),
        pltpu.VMEM((rows * slots, pairs), BF16),
        pltpu.VMEM((wide, pairs), F32),
        pltpu.VMEM((depth * n_emb, pairs), BF16),
        pltpu.VMEM((n_hi, depth, pairs), BF16),
        pltpu.VMEM((3, depth, pairs), BF16),
        pltpu.VMEM((3, depth, pairs), BF16),
        pltpu.VMEM((depth, pairs), BF16),
        pltpu.VMEM((rows * slots, wide), BF16),
        pltpu.VMEM((rows * slots, wide), BF16),
        pltpu.VMEM((n_emb, rows, 2 * LANES), BF16),
        pltpu.VMEM((pairs, 2 * LANES), BF16),
        pltpu.VMEM((chunk * n_group, LANES), BF16),
        pltpu.VMEM((n_group, chunk, LANES), BF16),
        pltpu.VMEM((piece * n_col, LANES), BF16),
        pltpu.VMEM((n_col, piece, LANES), BF16),
        pltpu.VMEM((piece * n_col, LANES), BF16),
        pltpu.VMEM((chunk * n_group, LANES), BF16),
    ]
    scratch.append(pltpu.SemaphoreType.DMA((3,)))
    for count in (n_emb, slots, 4, 4, n_hi, 4, 2, slots, n_emb, n_group, n_col, n_col, n_group):
        scratch += [pltpu.SemaphoreType.DMA((count,))] * 2
    hbm = pl.BlockSpec(memory_space=pltpu.HBM)
    smem = pl.BlockSpec(memory_space=pltpu.SMEM)
    vmem = pl.BlockSpec(memory_space=pltpu.VMEM)
    inputs = [
        pltpu.with_memory_space_constraint(x, pltpu.HBM)
        for x in (image_emb, text_feat, head_weight)
    ]
    image_grad, head_grad = pl.pallas_call(
        functools.partial(kernel, sizes),
        out_shape=(
            jax.ShapeDtypeStruct((depth, pairs), BF16),
            jax.ShapeDtypeStruct((depth, width), BF16),
        ),
        in_specs=[hbm, hbm, hbm, smem, smem],
        out_specs=(vmem, vmem),
        scratch_shapes=scratch,
        compiler_params=pltpu.CompilerParams(
            collective_id=0, has_side_effects=True, vmem_limit_bytes=40 * 1024 * 1024
        ),
    )(*inputs, logit_scale, logit_bias)
    return image_grad, head_grad.astype(F32)


def solution(mesh):
    placed = (P("emb", "dp"), P(None, "dp"), P("emb", None), P(), P())
    return jax.shard_map(
        on_device,
        mesh=mesh,
        in_specs=placed,
        out_specs=(P("emb", "dp"), P("emb", None)),
        check_vma=False,
    )
```

```python
import functools

import jax
import jax.numpy as jnp
from jax import lax
from jax.experimental import pallas as pl
from jax.experimental.pallas import tpu as pltpu
from jax.sharding import PartitionSpec as P

REACH = 6
EPSILON = 1e-06
N_ZLO, N_Y, N_X = 2, 8, 4
LANES = 128
ORDER = (0, 1, -1, 4, -4, 3, -3, 2, -2, 5, -5, 6, -6)
SLOT = {o: i for i, o in enumerate(ORDER)}
NEAR, MIDDLE = 7, 11
MESH = pl.DeviceIdType.MESH
BF16, F32 = jnp.bfloat16, jnp.float32


def up(value, step):
    return -(-value // step) * step


def kernel(
    sizes,
    image_hbm,
    feat_hbm,
    weight_hbm,
    scale_ref,
    bias_ref,
    image_out,
    head_out,
    image_ref,
    feat_ref,
    weight_ref,
    turn_f,
    swap_src,
    swap_dst,
    images,
    text_nat,
    text,
    weights,
    grad,
    text_part,
    pair_dst,
    line_src,
    line_dst,
    mid_dst,
    dirs,
    dirs_back,
    back_src,
    back_dst,
    head_src,
    head_dst,
    col_src,
    col_dst,
    col_sum,
    head_sum,
    load,
    swap_s,
    swap_r,
    win_s,
    win_r,
    gat_s,
    gat_r,
    fwd_s,
    fwd_r,
    pair_s,
    pair_r,
    line_s,
    line_r,
    mid_s,
    mid_r,
    ret_s,
    ret_r,
    back_s,
    back_r,
    head_s,
    head_r,
    col_s,
    col_r,
    cga_s,
    cga_r,
    hga_s,
    hga_r,
):
    n_dp, n_emb, depth, pairs, width, chunk, piece = sizes
    tail = depth - LANES
    rows = pairs // n_emb
    n_hi = n_emb // 2
    n_group, n_col = N_ZLO * N_X, N_Y
    wide = LANES * n_emb + LANES
    slots = 2 * REACH + 1
    me = lax.axis_index("dp")
    k = lax.axis_index("emb")
    hi, core = k // 2, k % 2
    x_at, y_at, z_at = me % N_X, (me // N_X) % N_Y, me // (N_X * N_Y)
    first_group = (z_at * N_X + x_at) * (1 - core) + y_at * core
    second_group = y_at * (1 - core) + (z_at * N_X + x_at) * core

    def emb_peer(m):
        return (me, (k + m) % n_emb)

    def dp_peer(offset):
        return ((me + offset + n_dp) % n_dp, k)

    partner = (me, k + 1 - 2 * core)

    def hi_of(m):
        return (hi + m) % n_hi

    def line_peer(m):
        return (me, 2 * hi_of(m) + core)

    def chip_at(plane, line):
        return (plane // N_X) * (N_X * N_Y) + line * N_X + plane % N_X

    def group_of(m):
        return (first_group + m) % n_group

    def group_peer(m):
        to = group_of(m)
        here, there = chip_at(to, y_at), chip_at(z_at * N_X + x_at, to)
        return (here * (1 - core) + there * core, k)

    def col_of(m):
        return (second_group + m) % n_col

    def col_peer(m):
        to = col_of(m)
        here, there = chip_at(z_at * N_X + x_at, to), chip_at(to, y_at)
        return (here * (1 - core) + there * core, k)

    def at16(start, size):
        return pl.ds(pl.multiple_of(start, 16), size)

    def push(src, dst, send, recv, peer):
        copy = pltpu.make_async_remote_copy(
            src_ref=src,
            dst_ref=dst,
            send_sem=send,
            recv_sem=recv,
            device_id=peer,
            device_id_type=MESH,
        )
        copy.start()
        return copy

    def slot(o):
        return pl.ds(rows * SLOT[o], rows)

    def loaded(i, src, dst):
        copy = pltpu.make_async_copy(src, dst, load.at[i])
        copy.start()
        return copy

    loads = [
        loaded(0, image_hbm, image_ref),
        loaded(1, weight_hbm, weight_ref),
        loaded(2, feat_hbm, feat_ref),
    ]

    greeted = (
        [emb_peer(m) for m in (4, 3, 5, 2, 6, 1, 7)]
        + [dp_peer(o) for o in (1, -1, N_X, -N_X, N_X - 1, 1 - N_X, N_X + 1, -N_X - 1)]
        + [group_peer(m) for m in range(1, n_group)]
        + [col_peer(m) for m in range(1, n_col)]
    )
    barrier = pltpu.get_barrier_semaphore()
    for peer in greeted:
        pl.semaphore_signal(barrier, inc=1, device_id=peer, device_id_type=MESH)

    per = LANES // rows
    loads[0].wait()
    turned = jnp.transpose(image_ref[:LANES, :].astype(F32)).astype(BF16)
    for j in range(n_emb):
        swap_src[j, :rows, :] = turned[rows * j : rows * (j + 1)]
        at = LANES * (j // per)
        swap_src[j, rows:, :] = image_ref[LANES:, at : at + LANES]
    swap_dst[pl.ds(k, 1)] = swap_src[pl.ds(k, 1)]
    own_text = at16(depth * k, depth)
    loads[1].wait()
    loads[2].wait()
    text_nat[own_text, :] = jnp.dot(
        weight_ref[...], feat_ref[...], preferred_element_type=F32
    ).astype(BF16)

    pl.semaphore_wait(barrier, len(greeted))

    swaps = [
        push(
            swap_src.at[(k + m) % n_emb],
            swap_dst.at[k],
            swap_s.at[m],
            swap_r.at[m],
            emb_peer(m),
        )
        for m in range(1, n_emb)
    ]
    upper, lower = line_peer(1), line_peer(n_hi - 1)
    cut = up(depth // 2, 16)
    below_to = depth * (2 * ((hi + n_hi - 1) % n_hi) + core)
    above_to = depth * (2 * ((hi + 1) % n_hi) + core)

    def text_push(start, size, i, peer):
        at = at16(start, size)
        return push(text_nat.at[at, :], text_nat.at[at, :], gat_s.at[i], gat_r.at[i], peer)

    gathers = [
        text_push(depth * k, cut, 0, upper),
        text_push(depth * k + cut, depth - cut, 1, lower),
        text_push(depth * k + cut, depth - cut, 2, upper),
        text_push(depth * k, cut, 3, lower),
    ]
    forwards = [
        push(text_nat.at[own_text, :], text_nat.at[own_text, :], fwd_s.at[0], fwd_r.at[0], partner)
    ]

    for copy in swaps:
        copy.wait_recv()
    raw = [swap_dst[j, :rows, :].astype(F32) for j in range(n_emb)]
    tails = jnp.concatenate([swap_dst[j, rows:, :].astype(F32) for j in range(n_emb)], axis=0)
    turn_f[:LANES, :LANES] = jnp.transpose(tails)
    raw.append(turn_f[at16(rows * (k % per), rows), :LANES])
    square = sum(jnp.sum(r * r, axis=1, keepdims=True) for r in raw)
    image_inv = 1.0 / jnp.sqrt(square + EPSILON)
    home = slot(0)
    for j, r in enumerate(raw):
        images[home, LANES * j : LANES * (j + 1)] = (r * image_inv).astype(BF16)
    window = {}

    def pass_on(have, o):
        window[o] = push(
            images.at[slot(have), :],
            images.at[slot(o), :],
            win_s.at[SLOT[o]],
            win_r.at[SLOT[o]],
            dp_peer(have - o),
        )

    for o in (1, -1, N_X, -N_X, N_X - 1, 1 - N_X):
        pass_on(0, o)

    gathers[0].wait_recv()
    gathers.append(text_push(below_to, cut, 4, upper))
    gathers[1].wait_recv()
    gathers.append(text_push(above_to + cut, depth - cut, 5, lower))
    for i, need, come in ((1, 2, below_to), (2, 3, above_to)):
        gathers[need].wait_recv()
        come = at16(come, depth)
        forwards.append(
            push(text_nat.at[come, :], text_nat.at[come, :], fwd_s.at[i], fwd_r.at[i], partner)
        )

    for near in (1, -1):
        window[near].wait_recv()
        for o in (N_X + 2, N_X + 1, 2):
            pass_on(near, near * o)

    gathers[4].wait_recv()
    gathers[5].wait_recv()
    come = at16(depth * (2 * ((hi + 2) % n_hi) + core), depth)
    forwards.append(
        push(text_nat.at[come, :], text_nat.at[come, :], fwd_s.at[3], fwd_r.at[3], partner)
    )

    for copy in forwards:
        copy.wait_recv()
    if LANES > tail * n_emb:
        text[LANES * n_emb + tail * n_emb :, :] = jnp.zeros((LANES - tail * n_emb, pairs), BF16)
    square = jnp.zeros((1, pairs), F32)
    for j in range(n_emb):
        part = text_nat[depth * j : depth * (j + 1), :]
        text[LANES * j : LANES * (j + 1), :] = part[:LANES]
        text[LANES * n_emb + tail * j : LANES * n_emb + tail * (j + 1), :] = part[LANES:]
        wide_part = part.astype(F32)
        square = square + jnp.sum(wide_part * wide_part, axis=0, keepdims=True)
    text_inv = 1.0 / jnp.sqrt(square + EPSILON)

    scale, bias = scale_ref[0], bias_ref[0]

    def meet(first, last):
        at = pl.ds(rows * first, rows * (last - first))
        cosine = jnp.dot(images[at, :], text[...], preferred_element_type=F32) * text_inv
        logits = scale * cosine + bias
        if first == 0:
            row_ids = lax.broadcasted_iota(jnp.int32, logits.shape, 0)
            col_ids = lax.broadcasted_iota(jnp.int32, logits.shape, 1)
            same = (row_ids < rows) & (col_ids - rows * k == row_ids)
            sign = jnp.where(same, jnp.float32(1.0), jnp.float32(-1.0))
        else:
            sign = jnp.float32(-1.0)
        sig = 1.0 / (1.0 + jnp.exp(sign * logits))
        value = (-scale * sign * sig * text_inv).astype(BF16)
        weights[at, :] = value
        return jnp.sum(value.astype(F32) * cosine, axis=0, keepdims=True)

    def turn_back(first, last):
        at = pl.ds(rows * first, rows * (last - first))
        dirs[at, :] = lax.dot_general(
            weights[at, :], text[...], (((1,), (1,)), ((), ())), preferred_element_type=F32
        ).astype(BF16)

    def text_side(first, last):
        at = pl.ds(rows * first, rows * (last - first))
        return lax.dot_general(
            images[at, :], weights[at, :], (((0,), (0,)), ((), ())), preferred_element_type=F32
        )

    for o in ORDER[3:NEAR]:
        window[o].wait_recv()
    inner = meet(0, NEAR)
    for o in ORDER[NEAR:MIDDLE]:
        window[o].wait_recv()
    inner = inner + meet(NEAR, MIDDLE)
    grad[...] = text_side(0, MIDDLE)
    for o in ORDER[MIDDLE:]:
        window[o].wait_recv()
    inner = (inner + meet(MIDDLE, len(ORDER))) * text_inv

    late = text_side(MIDDLE, len(ORDER))
    for j in range(n_emb):
        for at, size, to in ((LANES * j, LANES, 0), (LANES * n_emb + tail * j, tail, LANES)):
            part = grad[at : at + size, :] + late[at : at + size]
            part = part - text[at : at + size, :].astype(F32) * inner
            text_part[depth * j + to : depth * j + to + size, :] = part.astype(BF16)
    paired = {}
    for m in (2, 1, 3, 0):
        theirs = at16(depth * (2 * hi_of(m) + 1 - core), depth)
        paired[m] = push(text_part.at[theirs, :], pair_dst.at[m], pair_s.at[m], pair_r.at[m], partner)

    turn_back(0, len(ORDER))
    returns = {}

    def give_back(o, step):
        returns[o] = push(
            dirs.at[slot(o), :],
            dirs_back.at[slot(o), :],
            ret_s.at[SLOT[o]],
            ret_r.at[SLOT[o]],
            dp_peer(step),
        )

    def collect(o, sources):
        value = dirs[slot(o), :].astype(F32)
        for source in sources:
            returns[source].wait_recv()
            value = value + dirs_back[slot(source), :].astype(F32)
        return value

    def summed(m):
        paired[m].wait_recv()
        mine = at16(depth * (2 * hi_of(m) + core), depth)
        return text_part[mine, :].astype(F32) + pair_dst[m].astype(F32)

    first, second = pl.ds(0, cut), pl.ds(cut, depth - cut)
    line_src[0] = summed(2).astype(BF16)
    lines = [
        push(line_src.at[0, first, :], mid_dst.at[first, :], mid_s.at[0], mid_r.at[0], upper),
        push(line_src.at[0, second, :], mid_dst.at[second, :], mid_s.at[1], mid_r.at[1], lower),
    ]
    rising, falling = summed(1), summed(3)
    line_src[1, cut:, :] = rising[cut:].astype(BF16)
    line_src[2, :cut, :] = falling[:cut].astype(BF16)

    def line(i, j, part, peer):
        return push(line_src.at[i, part, :], line_dst.at[i, part, :], line_s.at[j], line_r.at[j], peer)

    lines.append(line(1, 0, second, upper))
    lines.append(line(2, 1, first, lower))
    lines[0].wait_recv()
    line_src[1, :cut, :] = (rising[:cut] + mid_dst[:cut, :].astype(F32)).astype(BF16)
    lines.append(line(1, 2, first, upper))
    lines[1].wait_recv()
    line_src[2, cut:, :] = (falling[cut:] + mid_dst[cut:, :].astype(F32)).astype(BF16)
    lines.append(line(2, 3, second, lower))
    for way in (1, -1):
        give_back(5 * way, N_X * way)
        give_back(3 * way, (N_X - 1) * way)
        give_back(6 * way, (N_X + 1) * way)
        give_back(2 * way, way)
        give_back(4 * way, N_X * way)
    for copy in swaps + gathers + forwards + list(window.values()):
        copy.wait_send()
    total = summed(0)
    for copy in lines[2:]:
        copy.wait_recv()
    total = total + line_dst[1].astype(F32) + line_dst[2].astype(F32)

    share = lax.dot_general(
        total.astype(BF16), feat_ref[...], (((1,), (1,)), ((), ())), preferred_element_type=F32
    )
    tiles = width // LANES
    for c in range(tiles):
        head_src[depth * c : depth * (c + 1), :] = share[:, LANES * c : LANES * (c + 1)].astype(BF16)
    if chunk * n_group > depth * tiles:
        head_src[depth * tiles :, :] = jnp.zeros((chunk * n_group - depth * tiles, LANES), BF16)
    heads = [
        push(
            head_src.at[at16(chunk * group_of(m), chunk), :],
            head_dst.at[m],
            head_s.at[m],
            head_r.at[m],
            group_peer(m),
        )
        for m in range(1, n_group)
    ]

    total = head_src[at16(chunk * first_group, chunk), :].astype(F32)
    for m in range(1, n_group):
        heads[m - 1].wait_recv()
        total = total + head_dst[m].astype(F32)
    col_src[:chunk, :] = total.astype(BF16)
    if piece * n_col > chunk:
        col_src[chunk:, :] = jnp.zeros((piece * n_col - chunk, LANES), BF16)
    cols = [
        push(col_src.at[at16(piece * col_of(m), piece), :], col_dst.at[m], col_s.at[m], col_r.at[m], col_peer(m))
        for m in range(1, n_col)
    ]

    for way in (1, -1):
        dirs[slot(way), :] = collect(way, (2 * way, 5 * way, 6 * way)).astype(BF16)
        give_back(way, way)

    own_piece = at16(piece * second_group, piece)
    total = col_src[own_piece, :].astype(F32)
    for m in range(1, n_col):
        cols[m - 1].wait_recv()
        total = total + col_dst[m].astype(F32)
    col_sum[own_piece, :] = total.astype(BF16)
    col_gathers = [
        push(col_sum.at[own_piece, :], col_sum.at[own_piece, :], cga_s.at[m], cga_r.at[m], col_peer(m))
        for m in range(1, n_col)
    ]

    for copy in lines + list(paired.values()) + heads:
        copy.wait_send()
    way = collect(0, (1, -1, 3, -3, 4, -4))
    unit = images[home, :].astype(F32)
    along = jnp.sum(unit * way, axis=1, keepdims=True)
    image_grad = ((way - unit * along) * image_inv).astype(BF16)
    for j in range(n_emb):
        back_src[j, :, :LANES] = image_grad[:, LANES * j : LANES * (j + 1)]
        back_src[j, :, LANES:] = image_grad[:, LANES * n_emb :]
    own_rows = at16(rows * k, rows)
    backs = [
        push(back_src.at[(k + m) % n_emb], back_dst.at[own_rows, :], back_s.at[m], back_r.at[m], emb_peer(m))
        for m in range(1, n_emb)
    ]
    back_dst[own_rows, :] = back_src[pl.ds(k, 1)][0]


    for copy in col_gathers:
        copy.wait_recv()
    own_chunk = at16(chunk * first_group, chunk)
    head_sum[own_chunk, :] = col_sum[:chunk, :]
    head_gathers = [
        push(col_sum.at[pl.ds(0, chunk), :], head_sum.at[own_chunk, :], hga_s.at[m], hga_r.at[m], group_peer(m))
        for m in range(1, n_group)
    ]

    for copy in backs:
        copy.wait_recv()
    turn_f[...] = jnp.transpose(back_dst[...].astype(F32))
    image_out[:LANES, :] = turn_f[:LANES, :].astype(BF16)
    image_out[LANES:, :] = turn_f[pl.ds(pl.multiple_of(LANES + tail * k, 16), tail), :].astype(BF16)

    for copy in list(returns.values()) + backs + cols + col_gathers:
        copy.wait_send()
    for copy in head_gathers:
        copy.wait_recv()
    for c in range(tiles):
        head_out[:, LANES * c : LANES * (c + 1)] = head_sum[depth * c : depth * (c + 1), :]

    for copy in head_gathers:
        copy.wait_send()


def on_device(image_emb, text_feat, head_weight, logit_scale, logit_bias):
    n_dp, n_emb = lax.axis_size("dp"), lax.axis_size("emb")
    depth, pairs = image_emb.shape
    width = text_feat.shape[0]
    rows = pairs // n_emb
    n_hi = n_emb // 2
    n_group, n_col = N_ZLO * N_X, N_Y
    slots = 2 * REACH + 1
    wide = LANES * n_emb + LANES
    chunk = up(depth * (width // LANES), 16 * n_group) // n_group
    piece = up(chunk, 16 * n_col) // n_col
    sizes = (n_dp, n_emb, depth, pairs, width, chunk, piece)
    scratch = [
        pltpu.VMEM((depth, pairs), BF16),
        pltpu.VMEM((width, pairs), BF16),
        pltpu.VMEM((depth, width), BF16),
        pltpu.VMEM((2 * LANES, pairs), F32),
        pltpu.VMEM((n_emb, rows + depth - LANES, LANES), BF16),
        pltpu.VMEM((n_emb, rows + depth - LANES, LANES), BF16),
        pltpu.VMEM((rows * slots, wide), BF16),
        pltpu.VMEM((depth * n_emb, pairs), BF16),
        pltpu.VMEM((wide, pairs), BF16),
        pltpu.VMEM((rows * slots, pairs), BF16),
        pltpu.VMEM((wide, pairs), F32),
        pltpu.VMEM((depth * n_emb, pairs), BF16),
        pltpu.VMEM((n_hi, depth, pairs), BF16),
        pltpu.VMEM((3, depth, pairs), BF16),
        pltpu.VMEM((3, depth, pairs), BF16),
        pltpu.VMEM((depth, pairs), BF16),
        pltpu.VMEM((rows * slots, wide), BF16),
        pltpu.VMEM((rows * slots, wide), BF16),
        pltpu.VMEM((n_emb, rows, 2 * LANES), BF16),
        pltpu.VMEM((pairs, 2 * LANES), BF16),
        pltpu.VMEM((chunk * n_group, LANES), BF16),
        pltpu.VMEM((n_group, chunk, LANES), BF16),
        pltpu.VMEM((piece * n_col, LANES), BF16),
        pltpu.VMEM((n_col, piece, LANES), BF16),
        pltpu.VMEM((piece * n_col, LANES), BF16),
        pltpu.VMEM((chunk * n_group, LANES), BF16),
    ]
    scratch.append(pltpu.SemaphoreType.DMA((3,)))
    for count in (n_emb, slots, 6, 4, n_hi, 4, 2, slots, n_emb, n_group, n_col, n_col, n_group):
        scratch += [pltpu.SemaphoreType.DMA((count,))] * 2
    hbm = pl.BlockSpec(memory_space=pltpu.HBM)
    smem = pl.BlockSpec(memory_space=pltpu.SMEM)
    vmem = pl.BlockSpec(memory_space=pltpu.VMEM)
    inputs = [
        pltpu.with_memory_space_constraint(x, pltpu.HBM)
        for x in (image_emb, text_feat, head_weight)
    ]
    image_grad, head_grad = pl.pallas_call(
        functools.partial(kernel, sizes),
        out_shape=(
            jax.ShapeDtypeStruct((depth, pairs), BF16),
            jax.ShapeDtypeStruct((depth, width), BF16),
        ),
        in_specs=[hbm, hbm, hbm, smem, smem],
        out_specs=(vmem, vmem),
        scratch_shapes=scratch,
        compiler_params=pltpu.CompilerParams(
            collective_id=0, has_side_effects=True, vmem_limit_bytes=40 * 1024 * 1024
        ),
    )(*inputs, logit_scale, logit_bias)
    return image_grad, head_grad.astype(F32)


def solution(mesh):
    placed = (P("emb", "dp"), P(None, "dp"), P("emb", None), P(), P())
    return jax.shard_map(
        on_device,
        mesh=mesh,
        in_specs=placed,
        out_specs=(P("emb", "dp"), P("emb", None)),
        check_vma=False,
    )
```

```python
import functools

import jax
import jax.numpy as jnp
from jax import lax
from jax.experimental import pallas as pl
from jax.experimental.pallas import tpu as pltpu
from jax.sharding import PartitionSpec as P

REACH = 6
EPSILON = 1e-06
N_ZLO, N_Y, N_X = 2, 8, 4
LANES = 128
ORDER = (0, 1, -1, 4, -4, 3, -3, 2, -2, 5, -5, 6, -6)
SLOT = {o: i for i, o in enumerate(ORDER)}
NEAR, MIDDLE = 7, 11
MESH = pl.DeviceIdType.MESH
BF16, F32 = jnp.bfloat16, jnp.float32


def up(value, step):
    return -(-value // step) * step


def kernel(
    sizes,
    image_hbm,
    feat_hbm,
    weight_hbm,
    scale_ref,
    bias_ref,
    image_out,
    head_out,
    image_ref,
    feat_ref,
    weight_ref,
    turn_f,
    swap_src,
    swap_dst,
    images,
    text_nat,
    text,
    weights,
    grad,
    text_part,
    pair_dst,
    line_src,
    line_dst,
    mid_dst,
    dirs,
    dirs_back,
    back_src,
    back_dst,
    head_src,
    head_dst,
    col_src,
    col_dst,
    col_sum,
    head_sum,
    load,
    swap_s,
    swap_r,
    win_s,
    win_r,
    gat_s,
    gat_r,
    fwd_s,
    fwd_r,
    pair_s,
    pair_r,
    line_s,
    line_r,
    mid_s,
    mid_r,
    ret_s,
    ret_r,
    back_s,
    back_r,
    head_s,
    head_r,
    col_s,
    col_r,
    cga_s,
    cga_r,
    hga_s,
    hga_r,
):
    n_dp, n_emb, depth, pairs, width, chunk, piece = sizes
    tail = depth - LANES
    rows = pairs // n_emb
    n_hi = n_emb // 2
    n_group, n_col = N_ZLO * N_X, N_Y
    wide = LANES * n_emb + LANES
    slots = 2 * REACH + 1
    me = lax.axis_index("dp")
    k = lax.axis_index("emb")
    hi, core = k // 2, k % 2
    x_at, y_at, z_at = me % N_X, (me // N_X) % N_Y, me // (N_X * N_Y)
    first_group = (z_at * N_X + x_at) * (1 - core) + y_at * core
    second_group = y_at * (1 - core) + (z_at * N_X + x_at) * core

    def emb_peer(m):
        return (me, (k + m) % n_emb)

    def dp_peer(offset):
        return ((me + offset + n_dp) % n_dp, k)

    partner = (me, k + 1 - 2 * core)

    def hi_of(m):
        return (hi + m) % n_hi

    def line_peer(m):
        return (me, 2 * hi_of(m) + core)

    def chip_at(plane, line):
        return (plane // N_X) * (N_X * N_Y) + line * N_X + plane % N_X

    plane_step = {4: 2, 3: 6, 5: 3, 2: 5, 6: 1, 1: 7, 7: 4}

    def group_of(m):
        return (first_group + plane_step[m] * (1 - core) + m * core) % n_group

    def group_peer(m):
        to = group_of(m)
        here, there = chip_at(to, y_at), chip_at(z_at * N_X + x_at, to)
        return (here * (1 - core) + there * core, k)

    def col_of(m):
        return (second_group + m * (1 - core) + plane_step[m] * core) % n_col

    def col_peer(m):
        to = col_of(m)
        here, there = chip_at(z_at * N_X + x_at, to), chip_at(to, y_at)
        return (here * (1 - core) + there * core, k)

    def at16(start, size):
        return pl.ds(pl.multiple_of(start, 16), size)

    def push(src, dst, send, recv, peer):
        copy = pltpu.make_async_remote_copy(
            src_ref=src,
            dst_ref=dst,
            send_sem=send,
            recv_sem=recv,
            device_id=peer,
            device_id_type=MESH,
        )
        copy.start()
        return copy

    def far_first(n):
        return sorted(range(1, n), key=lambda m: -min(m, n - m))

    def slot(o):
        return pl.ds(rows * SLOT[o], rows)

    def loaded(i, src, dst):
        copy = pltpu.make_async_copy(src, dst, load.at[i])
        copy.start()
        return copy

    loads = [
        loaded(0, image_hbm, image_ref),
        loaded(1, weight_hbm, weight_ref),
        loaded(2, feat_hbm, feat_ref),
    ]

    greeted = (
        [emb_peer(m) for m in far_first(n_emb)]
        + [dp_peer(o) for o in (1, -1, N_X, -N_X, N_X - 1, 1 - N_X, N_X + 1, -N_X - 1)]
        + [group_peer(m) for m in range(1, n_group)]
        + [col_peer(m) for m in range(1, n_col)]
    )
    barrier = pltpu.get_barrier_semaphore()
    for peer in greeted:
        pl.semaphore_signal(barrier, inc=1, device_id=peer, device_id_type=MESH)

    per = LANES // rows
    loads[0].wait()
    turned = jnp.transpose(image_ref[:LANES, :].astype(F32)).astype(BF16)
    for j in range(n_emb):
        swap_src[j, :rows, :] = turned[rows * j : rows * (j + 1)]
        at = LANES * (j // per)
        swap_src[j, rows:, :] = image_ref[LANES:, at : at + LANES]
    swap_dst[pl.ds(k, 1)] = swap_src[pl.ds(k, 1)]
    own_text = at16(depth * k, depth)
    loads[1].wait()
    loads[2].wait()
    text_nat[own_text, :] = jnp.dot(
        weight_ref[...], feat_ref[...], preferred_element_type=F32
    ).astype(BF16)

    pl.semaphore_wait(barrier, len(greeted))

    swaps = [
        push(
            swap_src.at[(k + m) % n_emb],
            swap_dst.at[k],
            swap_s.at[m],
            swap_r.at[m],
            emb_peer(m),
        )
        for m in far_first(n_emb)
    ]
    upper, lower = line_peer(1), line_peer(n_hi - 1)
    cut = up(depth // 2, 16)
    below_to = depth * (2 * ((hi + n_hi - 1) % n_hi) + core)
    above_to = depth * (2 * ((hi + 1) % n_hi) + core)

    def text_push(start, size, i, peer):
        at = at16(start, size)
        return push(text_nat.at[at, :], text_nat.at[at, :], gat_s.at[i], gat_r.at[i], peer)

    gathers = [
        text_push(depth * k, cut, 0, upper),
        text_push(depth * k + cut, depth - cut, 1, lower),
        text_push(depth * k + cut, depth - cut, 2, upper),
        text_push(depth * k, cut, 3, lower),
    ]
    forwards = [
        push(text_nat.at[own_text, :], text_nat.at[own_text, :], fwd_s.at[0], fwd_r.at[0], partner)
    ]

    for copy in swaps:
        copy.wait_recv()
    raw = [swap_dst[j, :rows, :].astype(F32) for j in range(n_emb)]
    tails = jnp.concatenate([swap_dst[j, rows:, :].astype(F32) for j in range(n_emb)], axis=0)
    turn_f[:LANES, :LANES] = jnp.transpose(tails)
    raw.append(turn_f[at16(rows * (k % per), rows), :LANES])
    square = sum(jnp.sum(r * r, axis=1, keepdims=True) for r in raw)
    image_inv = 1.0 / jnp.sqrt(square + EPSILON)
    home = slot(0)
    for j, r in enumerate(raw):
        images[home, LANES * j : LANES * (j + 1)] = (r * image_inv).astype(BF16)
    window = {}

    def pass_on(have, o):
        window[o] = push(
            images.at[slot(have), :],
            images.at[slot(o), :],
            win_s.at[SLOT[o]],
            win_r.at[SLOT[o]],
            dp_peer(have - o),
        )

    for o in (1, -1, N_X, -N_X, N_X - 1, 1 - N_X):
        pass_on(0, o)

    gathers[0].wait_recv()
    gathers.append(text_push(below_to, cut, 4, upper))
    gathers[1].wait_recv()
    gathers.append(text_push(above_to + cut, depth - cut, 5, lower))
    for i, need, come in ((1, 2, below_to), (2, 3, above_to)):
        gathers[need].wait_recv()
        come = at16(come, depth)
        forwards.append(
            push(text_nat.at[come, :], text_nat.at[come, :], fwd_s.at[i], fwd_r.at[i], partner)
        )

    for near in (1, -1):
        window[near].wait_recv()
        for o in (N_X + 2, N_X + 1, 2):
            pass_on(near, near * o)

    gathers[4].wait_recv()
    gathers[5].wait_recv()
    come = at16(depth * (2 * ((hi + 2) % n_hi) + core), depth)
    forwards.append(
        push(text_nat.at[come, :], text_nat.at[come, :], fwd_s.at[3], fwd_r.at[3], partner)
    )

    for copy in forwards:
        copy.wait_recv()
    if LANES > tail * n_emb:
        text[LANES * n_emb + tail * n_emb :, :] = jnp.zeros((LANES - tail * n_emb, pairs), BF16)
    square = jnp.zeros((1, pairs), F32)
    for j in range(n_emb):
        part = text_nat[depth * j : depth * (j + 1), :]
        text[LANES * j : LANES * (j + 1), :] = part[:LANES]
        text[LANES * n_emb + tail * j : LANES * n_emb + tail * (j + 1), :] = part[LANES:]
        wide_part = part.astype(F32)
        square = square + jnp.sum(wide_part * wide_part, axis=0, keepdims=True)
    text_inv = 1.0 / jnp.sqrt(square + EPSILON)

    scale, bias = scale_ref[0], bias_ref[0]

    def meet(first, last):
        at = pl.ds(rows * first, rows * (last - first))
        cosine = jnp.dot(images[at, :], text[...], preferred_element_type=F32) * text_inv
        logits = scale * cosine + bias
        if first == 0:
            row_ids = lax.broadcasted_iota(jnp.int32, logits.shape, 0)
            col_ids = lax.broadcasted_iota(jnp.int32, logits.shape, 1)
            same = (row_ids < rows) & (col_ids - rows * k == row_ids)
            sign = jnp.where(same, jnp.float32(1.0), jnp.float32(-1.0))
        else:
            sign = jnp.float32(-1.0)
        sig = 1.0 / (1.0 + jnp.exp(sign * logits))
        value = (-scale * sign * sig * text_inv).astype(BF16)
        weights[at, :] = value
        return jnp.sum(value.astype(F32) * cosine, axis=0, keepdims=True)

    def turn_back(first, last):
        at = pl.ds(rows * first, rows * (last - first))
        dirs[at, :] = lax.dot_general(
            weights[at, :], text[...], (((1,), (1,)), ((), ())), preferred_element_type=F32
        ).astype(BF16)

    def text_side(first, last):
        at = pl.ds(rows * first, rows * (last - first))
        return lax.dot_general(
            images[at, :], weights[at, :], (((0,), (0,)), ((), ())), preferred_element_type=F32
        )

    returns = {}

    def give_back(o, step):
        returns[o] = push(
            dirs.at[slot(o), :],
            dirs_back.at[slot(o), :],
            ret_s.at[SLOT[o]],
            ret_r.at[SLOT[o]],
            dp_peer(step),
        )

    def collect(o, sources):
        value = dirs[slot(o), :].astype(F32)
        for source in sources:
            returns[source].wait_recv()
            value = value + dirs_back[slot(source), :].astype(F32)
        return value

    for o in ORDER[3:NEAR]:
        window[o].wait_recv()
    inner = meet(0, NEAR)
    turn_back(0, NEAR)
    for way in (1, -1):
        give_back(4 * way, N_X * way)
        give_back(3 * way, (N_X - 1) * way)
    for o in ORDER[NEAR:MIDDLE]:
        window[o].wait_recv()
    inner = inner + meet(NEAR, MIDDLE)
    grad[...] = text_side(0, MIDDLE)
    for o in ORDER[MIDDLE:]:
        window[o].wait_recv()
    inner = (inner + meet(MIDDLE, len(ORDER))) * text_inv

    late = text_side(MIDDLE, len(ORDER))
    for j in range(n_emb):
        for at, size, to in ((LANES * j, LANES, 0), (LANES * n_emb + tail * j, tail, LANES)):
            part = grad[at : at + size, :] + late[at : at + size]
            part = part - text[at : at + size, :].astype(F32) * inner
            text_part[depth * j + to : depth * j + to + size, :] = part.astype(BF16)
    paired = {}
    for m in (2, 1, 3, 0):
        theirs = at16(depth * (2 * hi_of(m) + 1 - core), depth)
        paired[m] = push(text_part.at[theirs, :], pair_dst.at[m], pair_s.at[m], pair_r.at[m], partner)

    turn_back(NEAR, len(ORDER))
    def summed(m):
        paired[m].wait_recv()
        mine = at16(depth * (2 * hi_of(m) + core), depth)
        return text_part[mine, :].astype(F32) + pair_dst[m].astype(F32)

    first, second = pl.ds(0, cut), pl.ds(cut, depth - cut)
    line_src[0] = summed(2).astype(BF16)
    lines = [
        push(line_src.at[0, first, :], mid_dst.at[first, :], mid_s.at[0], mid_r.at[0], upper),
        push(line_src.at[0, second, :], mid_dst.at[second, :], mid_s.at[1], mid_r.at[1], lower),
    ]
    rising, falling = summed(1), summed(3)
    line_src[1, cut:, :] = rising[cut:].astype(BF16)
    line_src[2, :cut, :] = falling[:cut].astype(BF16)

    def line(i, j, part, peer):
        return push(line_src.at[i, part, :], line_dst.at[i, part, :], line_s.at[j], line_r.at[j], peer)

    lines.append(line(1, 0, second, upper))
    lines.append(line(2, 1, first, lower))
    lines[0].wait_recv()
    line_src[1, :cut, :] = (rising[:cut] + mid_dst[:cut, :].astype(F32)).astype(BF16)
    lines.append(line(1, 2, first, upper))
    lines[1].wait_recv()
    line_src[2, cut:, :] = (falling[cut:] + mid_dst[cut:, :].astype(F32)).astype(BF16)
    lines.append(line(2, 3, second, lower))
    for way in (1, -1):
        give_back(5 * way, N_X * way)
        give_back(6 * way, (N_X + 1) * way)
        give_back(2 * way, way)
    for copy in swaps + gathers + forwards + list(window.values()):
        copy.wait_send()
    total = summed(0)
    for copy in lines[2:]:
        copy.wait_recv()
    total = total + line_dst[1].astype(F32) + line_dst[2].astype(F32)

    share = lax.dot_general(
        total.astype(BF16), feat_ref[...], (((1,), (1,)), ((), ())), preferred_element_type=F32
    )
    tiles = width // LANES
    for c in range(tiles):
        head_src[depth * c : depth * (c + 1), :] = share[:, LANES * c : LANES * (c + 1)].astype(BF16)
    if chunk * n_group > depth * tiles:
        head_src[depth * tiles :, :] = jnp.zeros((chunk * n_group - depth * tiles, LANES), BF16)
    heads = [
        push(
            head_src.at[at16(chunk * group_of(m), chunk), :],
            head_dst.at[m],
            head_s.at[m],
            head_r.at[m],
            group_peer(m),
        )
        for m in far_first(n_group)
    ]

    total = head_src[at16(chunk * first_group, chunk), :].astype(F32)
    for m, copy in zip(far_first(n_group), heads):
        copy.wait_recv()
        total = total + head_dst[m].astype(F32)
    col_src[:chunk, :] = total.astype(BF16)
    if piece * n_col > chunk:
        col_src[chunk:, :] = jnp.zeros((piece * n_col - chunk, LANES), BF16)
    cols = [
        push(col_src.at[at16(piece * col_of(m), piece), :], col_dst.at[m], col_s.at[m], col_r.at[m], col_peer(m))
        for m in far_first(n_col)
    ]

    for way in (1, -1):
        dirs[slot(way), :] = collect(way, (2 * way, 5 * way, 6 * way)).astype(BF16)
        give_back(way, way)

    own_piece = at16(piece * second_group, piece)
    total = col_src[own_piece, :].astype(F32)
    for m, copy in zip(far_first(n_col), cols):
        copy.wait_recv()
        total = total + col_dst[m].astype(F32)
    col_sum[own_piece, :] = total.astype(BF16)
    col_gathers = [
        push(col_sum.at[own_piece, :], col_sum.at[own_piece, :], cga_s.at[m], cga_r.at[m], col_peer(m))
        for m in far_first(n_col)
    ]

    for copy in lines + list(paired.values()) + heads:
        copy.wait_send()
    way = collect(0, (1, -1, 3, -3, 4, -4))
    unit = images[home, :].astype(F32)
    along = jnp.sum(unit * way, axis=1, keepdims=True)
    image_grad = ((way - unit * along) * image_inv).astype(BF16)
    for j in range(n_emb):
        back_src[j, :, :LANES] = image_grad[:, LANES * j : LANES * (j + 1)]
        back_src[j, :, LANES:] = image_grad[:, LANES * n_emb :]
    own_rows = at16(rows * k, rows)
    backs = [
        push(back_src.at[(k + m) % n_emb], back_dst.at[own_rows, :], back_s.at[m], back_r.at[m], emb_peer(m))
        for m in far_first(n_emb)
    ]
    back_dst[own_rows, :] = back_src[pl.ds(k, 1)][0]


    for copy in col_gathers:
        copy.wait_recv()
    own_chunk = at16(chunk * first_group, chunk)
    head_sum[own_chunk, :] = col_sum[:chunk, :]
    head_gathers = [
        push(col_sum.at[pl.ds(0, chunk), :], head_sum.at[own_chunk, :], hga_s.at[m], hga_r.at[m], group_peer(m))
        for m in far_first(n_group)
    ]

    for copy in backs:
        copy.wait_recv()
    turn_f[...] = jnp.transpose(back_dst[...].astype(F32))
    image_out[:LANES, :] = turn_f[:LANES, :].astype(BF16)
    image_out[LANES:, :] = turn_f[pl.ds(pl.multiple_of(LANES + tail * k, 16), tail), :].astype(BF16)

    for copy in list(returns.values()) + backs + cols + col_gathers:
        copy.wait_send()
    for copy in head_gathers:
        copy.wait_recv()
    for c in range(tiles):
        head_out[:, LANES * c : LANES * (c + 1)] = head_sum[depth * c : depth * (c + 1), :]

    for copy in head_gathers:
        copy.wait_send()


def on_device(image_emb, text_feat, head_weight, logit_scale, logit_bias):
    n_dp, n_emb = lax.axis_size("dp"), lax.axis_size("emb")
    depth, pairs = image_emb.shape
    width = text_feat.shape[0]
    rows = pairs // n_emb
    n_hi = n_emb // 2
    n_group, n_col = N_ZLO * N_X, N_Y
    slots = 2 * REACH + 1
    wide = LANES * n_emb + LANES
    chunk = up(depth * (width // LANES), 16 * n_group) // n_group
    piece = up(chunk, 16 * n_col) // n_col
    sizes = (n_dp, n_emb, depth, pairs, width, chunk, piece)
    scratch = [
        pltpu.VMEM((depth, pairs), BF16),
        pltpu.VMEM((width, pairs), BF16),
        pltpu.VMEM((depth, width), BF16),
        pltpu.VMEM((2 * LANES, pairs), F32),
        pltpu.VMEM((n_emb, rows + depth - LANES, LANES), BF16),
        pltpu.VMEM((n_emb, rows + depth - LANES, LANES), BF16),
        pltpu.VMEM((rows * slots, wide), BF16),
        pltpu.VMEM((depth * n_emb, pairs), BF16),
        pltpu.VMEM((wide, pairs), BF16),
        pltpu.VMEM((rows * slots, pairs), BF16),
        pltpu.VMEM((wide, pairs), F32),
        pltpu.VMEM((depth * n_emb, pairs), BF16),
        pltpu.VMEM((n_hi, depth, pairs), BF16),
        pltpu.VMEM((3, depth, pairs), BF16),
        pltpu.VMEM((3, depth, pairs), BF16),
        pltpu.VMEM((depth, pairs), BF16),
        pltpu.VMEM((rows * slots, wide), BF16),
        pltpu.VMEM((rows * slots, wide), BF16),
        pltpu.VMEM((n_emb, rows, 2 * LANES), BF16),
        pltpu.VMEM((pairs, 2 * LANES), BF16),
        pltpu.VMEM((chunk * n_group, LANES), BF16),
        pltpu.VMEM((n_group, chunk, LANES), BF16),
        pltpu.VMEM((piece * n_col, LANES), BF16),
        pltpu.VMEM((n_col, piece, LANES), BF16),
        pltpu.VMEM((piece * n_col, LANES), BF16),
        pltpu.VMEM((chunk * n_group, LANES), BF16),
    ]
    scratch.append(pltpu.SemaphoreType.DMA((3,)))
    for count in (n_emb, slots, 6, 4, n_hi, 4, 2, slots, n_emb, n_group, n_col, n_col, n_group):
        scratch += [pltpu.SemaphoreType.DMA((count,))] * 2
    hbm = pl.BlockSpec(memory_space=pltpu.HBM)
    smem = pl.BlockSpec(memory_space=pltpu.SMEM)
    vmem = pl.BlockSpec(memory_space=pltpu.VMEM)
    inputs = [
        pltpu.with_memory_space_constraint(x, pltpu.HBM)
        for x in (image_emb, text_feat, head_weight)
    ]
    image_grad, head_grad = pl.pallas_call(
        functools.partial(kernel, sizes),
        out_shape=(
            jax.ShapeDtypeStruct((depth, pairs), BF16),
            jax.ShapeDtypeStruct((depth, width), BF16),
        ),
        in_specs=[hbm, hbm, hbm, smem, smem],
        out_specs=(vmem, vmem),
        scratch_shapes=scratch,
        compiler_params=pltpu.CompilerParams(
            collective_id=0, has_side_effects=True, vmem_limit_bytes=40 * 1024 * 1024
        ),
    )(*inputs, logit_scale, logit_bias)
    return image_grad, head_grad.astype(F32)


def solution(mesh):
    placed = (P("emb", "dp"), P(None, "dp"), P("emb", None), P(), P())
    return jax.shard_map(
        on_device,
        mesh=mesh,
        in_specs=placed,
        out_specs=(P("emb", "dp"), P("emb", None)),
        check_vma=False,
    )
```

```python
import functools

import jax
import jax.numpy as jnp
from jax import lax
from jax.experimental import pallas as pl
from jax.experimental.pallas import tpu as pltpu
from jax.sharding import PartitionSpec as P

REACH = 6
EPSILON = 1e-06
N_ZLO, N_Y, N_X = 2, 8, 4
LANES = 128
ORDER = (0, 1, -1, 4, -4, 3, -3, 2, -2, 5, -5, 6, -6)
SLOT = {o: i for i, o in enumerate(ORDER)}
NEAR, MIDDLE = 7, 11
MESH = pl.DeviceIdType.MESH
BF16, F32 = jnp.bfloat16, jnp.float32


def up(value, step):
    return -(-value // step) * step


def kernel(
    sizes,
    image_hbm,
    feat_hbm,
    weight_hbm,
    scale_ref,
    bias_ref,
    image_out,
    head_out,
    image_ref,
    feat_ref,
    weight_ref,
    turn_f,
    swap_src,
    swap_dst,
    images,
    text_nat,
    text,
    weights,
    grad,
    text_part,
    pair_dst,
    line_src,
    line_dst,
    mid_dst,
    dirs,
    dirs_back,
    back_src,
    back_dst,
    head_src,
    head_dst,
    col_src,
    col_dst,
    col_sum,
    head_sum,
    load,
    swap_s,
    swap_r,
    win_s,
    win_r,
    gat_s,
    gat_r,
    fwd_s,
    fwd_r,
    pair_s,
    pair_r,
    line_s,
    line_r,
    mid_s,
    mid_r,
    ret_s,
    ret_r,
    back_s,
    back_r,
    head_s,
    head_r,
    col_s,
    col_r,
    cga_s,
    cga_r,
    hga_s,
    hga_r,
):
    n_dp, n_emb, depth, pairs, width, chunk, piece = sizes
    tail = depth - LANES
    rows = pairs // n_emb
    n_hi = n_emb // 2
    n_group, n_col = N_ZLO * N_X, N_Y
    wide = LANES * n_emb + LANES
    slots = 2 * REACH + 1
    me = lax.axis_index("dp")
    k = lax.axis_index("emb")
    hi, core = k // 2, k % 2
    x_at, y_at, z_at = me % N_X, (me // N_X) % N_Y, me // (N_X * N_Y)
    first_group = (z_at * N_X + x_at) * (1 - core) + y_at * core
    second_group = y_at * (1 - core) + (z_at * N_X + x_at) * core

    def emb_peer(m):
        return (me, (k + m) % n_emb)

    def dp_peer(offset):
        return ((me + offset + n_dp) % n_dp, k)

    partner = (me, k + 1 - 2 * core)

    def hi_of(m):
        return (hi + m) % n_hi

    def line_peer(m):
        return (me, 2 * hi_of(m) + core)

    def chip_at(plane, line):
        return (plane // N_X) * (N_X * N_Y) + line * N_X + plane % N_X

    plane_step = {4: 2, 3: 6, 5: 3, 2: 5, 6: 1, 1: 7, 7: 4}

    def group_of(m):
        return (first_group + plane_step[m] * (1 - core) + m * core) % n_group

    def group_peer(m):
        to = group_of(m)
        here, there = chip_at(to, y_at), chip_at(z_at * N_X + x_at, to)
        return (here * (1 - core) + there * core, k)

    def col_of(m):
        return (second_group + m * (1 - core) + plane_step[m] * core) % n_col

    def col_peer(m):
        to = col_of(m)
        here, there = chip_at(z_at * N_X + x_at, to), chip_at(to, y_at)
        return (here * (1 - core) + there * core, k)

    def at16(start, size):
        return pl.ds(pl.multiple_of(start, 16), size)

    def push(src, dst, send, recv, peer):
        copy = pltpu.make_async_remote_copy(
            src_ref=src,
            dst_ref=dst,
            send_sem=send,
            recv_sem=recv,
            device_id=peer,
            device_id_type=MESH,
        )
        copy.start()
        return copy

    def far_first(n):
        return sorted(range(1, n), key=lambda m: -min(m, n - m))

    def slot(o):
        return pl.ds(rows * SLOT[o], rows)

    def loaded(i, src, dst):
        copy = pltpu.make_async_copy(src, dst, load.at[i])
        copy.start()
        return copy

    loads = [
        loaded(0, image_hbm, image_ref),
        loaded(1, weight_hbm, weight_ref),
        loaded(2, feat_hbm, feat_ref),
    ]

    greeted = (
        [emb_peer(m) for m in far_first(n_emb)]
        + [dp_peer(o) for o in (1, -1, N_X, -N_X, N_X - 1, 1 - N_X, N_X + 1, -N_X - 1)]
        + [group_peer(m) for m in range(1, n_group)]
        + [col_peer(m) for m in range(1, n_col)]
    )
    barrier = pltpu.get_barrier_semaphore()
    for peer in greeted:
        pl.semaphore_signal(barrier, inc=1, device_id=peer, device_id_type=MESH)

    per = LANES // rows
    loads[0].wait()
    turned = jnp.transpose(image_ref[:LANES, :].astype(F32)).astype(BF16)
    for j in range(n_emb):
        swap_src[j, :rows, :] = turned[rows * j : rows * (j + 1)]
        at = LANES * (j // per)
        swap_src[j, rows:, :] = image_ref[LANES:, at : at + LANES]
    swap_dst[pl.ds(k, 1)] = swap_src[pl.ds(k, 1)]
    own_text = at16(depth * k, depth)
    loads[1].wait()
    loads[2].wait()
    text_nat[own_text, :] = jnp.dot(
        weight_ref[...], feat_ref[...], preferred_element_type=F32
    ).astype(BF16)

    pl.semaphore_wait(barrier, len(greeted))

    swaps = [
        push(
            swap_src.at[(k + m) % n_emb],
            swap_dst.at[k],
            swap_s.at[m],
            swap_r.at[m],
            emb_peer(m),
        )
        for m in far_first(n_emb)
    ]
    upper, lower = line_peer(1), line_peer(n_hi - 1)
    cut = up(depth // 2, 16)
    below_to = depth * (2 * ((hi + n_hi - 1) % n_hi) + core)
    above_to = depth * (2 * ((hi + 1) % n_hi) + core)

    def text_push(start, size, i, peer):
        at = at16(start, size)
        return push(text_nat.at[at, :], text_nat.at[at, :], gat_s.at[i], gat_r.at[i], peer)

    gathers = [
        text_push(depth * k, cut, 0, upper),
        text_push(depth * k + cut, depth - cut, 1, lower),
        text_push(depth * k + cut, depth - cut, 2, upper),
        text_push(depth * k, cut, 3, lower),
    ]
    forwards = [
        push(text_nat.at[own_text, :], text_nat.at[own_text, :], fwd_s.at[0], fwd_r.at[0], partner)
    ]

    for copy in swaps:
        copy.wait_recv()
    raw = [swap_dst[j, :rows, :].astype(F32) for j in range(n_emb)]
    tails = jnp.concatenate([swap_dst[j, rows:, :].astype(F32) for j in range(n_emb)], axis=0)
    turn_f[:LANES, :LANES] = jnp.transpose(tails)
    raw.append(turn_f[at16(rows * (k % per), rows), :LANES])
    square = sum(jnp.sum(r * r, axis=1, keepdims=True) for r in raw)
    image_inv = 1.0 / jnp.sqrt(square + EPSILON)
    home = slot(0)
    for j, r in enumerate(raw):
        images[home, LANES * j : LANES * (j + 1)] = (r * image_inv).astype(BF16)
    window = {}

    def pass_on(have, o):
        window[o] = push(
            images.at[slot(have), :],
            images.at[slot(o), :],
            win_s.at[SLOT[o]],
            win_r.at[SLOT[o]],
            dp_peer(have - o),
        )

    for o in (1, -1, N_X, -N_X, N_X - 1, 1 - N_X):
        pass_on(0, o)

    gathers[0].wait_recv()
    gathers.append(text_push(below_to, cut, 4, upper))
    gathers[1].wait_recv()
    gathers.append(text_push(above_to + cut, depth - cut, 5, lower))
    for i, need, come in ((1, 2, below_to), (2, 3, above_to)):
        gathers[need].wait_recv()
        come = at16(come, depth)
        forwards.append(
            push(text_nat.at[come, :], text_nat.at[come, :], fwd_s.at[i], fwd_r.at[i], partner)
        )

    for near in (1, -1):
        window[near].wait_recv()
        for o in (N_X + 2, N_X + 1, 2):
            pass_on(near, near * o)

    gathers[4].wait_recv()
    gathers[5].wait_recv()
    come = at16(depth * (2 * ((hi + 2) % n_hi) + core), depth)
    forwards.append(
        push(text_nat.at[come, :], text_nat.at[come, :], fwd_s.at[3], fwd_r.at[3], partner)
    )

    for copy in forwards:
        copy.wait_recv()
    if LANES > tail * n_emb:
        text[LANES * n_emb + tail * n_emb :, :] = jnp.zeros((LANES - tail * n_emb, pairs), BF16)
    square = jnp.zeros((1, pairs), F32)
    for j in range(n_emb):
        part = text_nat[depth * j : depth * (j + 1), :]
        text[LANES * j : LANES * (j + 1), :] = part[:LANES]
        text[LANES * n_emb + tail * j : LANES * n_emb + tail * (j + 1), :] = part[LANES:]
        wide_part = part.astype(F32)
        square = square + jnp.sum(wide_part * wide_part, axis=0, keepdims=True)
    text_inv = 1.0 / jnp.sqrt(square + EPSILON)

    scale, bias = scale_ref[0], bias_ref[0]

    def meet(first, last):
        at = pl.ds(rows * first, rows * (last - first))
        cosine = jnp.dot(images[at, :], text[...], preferred_element_type=F32) * text_inv
        logits = scale * cosine + bias
        if first == 0:
            row_ids = lax.broadcasted_iota(jnp.int32, logits.shape, 0)
            col_ids = lax.broadcasted_iota(jnp.int32, logits.shape, 1)
            same = (row_ids < rows) & (col_ids - rows * k == row_ids)
            sign = jnp.where(same, jnp.float32(1.0), jnp.float32(-1.0))
        else:
            sign = jnp.float32(-1.0)
        sig = 1.0 / (1.0 + jnp.exp(sign * logits))
        value = (-scale * sign * sig * text_inv).astype(BF16)
        weights[at, :] = value
        return jnp.sum(value.astype(F32) * cosine, axis=0, keepdims=True)

    def turn_back(first, last):
        at = pl.ds(rows * first, rows * (last - first))
        dirs[at, :] = lax.dot_general(
            weights[at, :], text[...], (((1,), (1,)), ((), ())), preferred_element_type=F32
        ).astype(BF16)

    def text_side(first, last):
        at = pl.ds(rows * first, rows * (last - first))
        return lax.dot_general(
            images[at, :], weights[at, :], (((0,), (0,)), ((), ())), preferred_element_type=F32
        )

    returns = {}

    def give_back(o, step):
        returns[o] = push(
            dirs.at[slot(o), :],
            dirs_back.at[slot(o), :],
            ret_s.at[SLOT[o]],
            ret_r.at[SLOT[o]],
            dp_peer(step),
        )

    def collect(o, sources):
        value = dirs[slot(o), :].astype(F32)
        for source in sources:
            returns[source].wait_recv()
            value = value + dirs_back[slot(source), :].astype(F32)
        return value

    for o in ORDER[3:NEAR]:
        window[o].wait_recv()
    inner = meet(0, NEAR)
    turn_back(0, NEAR)
    for way in (1, -1):
        give_back(4 * way, N_X * way)
        give_back(3 * way, (N_X - 1) * way)
    for o in ORDER[NEAR:MIDDLE]:
        window[o].wait_recv()
    inner = inner + meet(NEAR, MIDDLE)
    turn_back(NEAR, MIDDLE)
    for way in (1, -1):
        give_back(5 * way, N_X * way)
        give_back(2 * way, way)
    grad[...] = text_side(0, MIDDLE)
    for o in ORDER[MIDDLE:]:
        window[o].wait_recv()
    inner = (inner + meet(MIDDLE, len(ORDER))) * text_inv

    late = text_side(MIDDLE, len(ORDER))
    for j in range(n_emb):
        for at, size, to in ((LANES * j, LANES, 0), (LANES * n_emb + tail * j, tail, LANES)):
            part = grad[at : at + size, :] + late[at : at + size]
            part = part - text[at : at + size, :].astype(F32) * inner
            text_part[depth * j + to : depth * j + to + size, :] = part.astype(BF16)
    paired = {}
    for m in (2, 1, 3, 0):
        theirs = at16(depth * (2 * hi_of(m) + 1 - core), depth)
        paired[m] = push(text_part.at[theirs, :], pair_dst.at[m], pair_s.at[m], pair_r.at[m], partner)

    turn_back(MIDDLE, len(ORDER))

    def summed(m):
        paired[m].wait_recv()
        mine = at16(depth * (2 * hi_of(m) + core), depth)
        return text_part[mine, :].astype(F32) + pair_dst[m].astype(F32)

    first, second = pl.ds(0, cut), pl.ds(cut, depth - cut)
    line_src[0] = summed(2).astype(BF16)
    lines = [
        push(line_src.at[0, first, :], mid_dst.at[first, :], mid_s.at[0], mid_r.at[0], upper),
        push(line_src.at[0, second, :], mid_dst.at[second, :], mid_s.at[1], mid_r.at[1], lower),
    ]
    rising, falling = summed(1), summed(3)
    line_src[1, cut:, :] = rising[cut:].astype(BF16)
    line_src[2, :cut, :] = falling[:cut].astype(BF16)

    def line(i, j, part, peer):
        return push(line_src.at[i, part, :], line_dst.at[i, part, :], line_s.at[j], line_r.at[j], peer)

    lines.append(line(1, 0, second, upper))
    lines.append(line(2, 1, first, lower))
    lines[0].wait_recv()
    line_src[1, :cut, :] = (rising[:cut] + mid_dst[:cut, :].astype(F32)).astype(BF16)
    lines.append(line(1, 2, first, upper))
    lines[1].wait_recv()
    line_src[2, cut:, :] = (falling[cut:] + mid_dst[cut:, :].astype(F32)).astype(BF16)
    lines.append(line(2, 3, second, lower))
    for way in (1, -1):
        give_back(6 * way, (N_X + 1) * way)
    for copy in swaps + gathers + forwards + list(window.values()):
        copy.wait_send()
    total = summed(0)
    for copy in lines[2:]:
        copy.wait_recv()
    total = total + line_dst[1].astype(F32) + line_dst[2].astype(F32)

    share = lax.dot_general(
        total.astype(BF16), feat_ref[...], (((1,), (1,)), ((), ())), preferred_element_type=F32
    )
    tiles = width // LANES
    for c in range(tiles):
        head_src[depth * c : depth * (c + 1), :] = share[:, LANES * c : LANES * (c + 1)].astype(BF16)
    if chunk * n_group > depth * tiles:
        head_src[depth * tiles :, :] = jnp.zeros((chunk * n_group - depth * tiles, LANES), BF16)
    heads = [
        push(
            head_src.at[at16(chunk * group_of(m), chunk), :],
            head_dst.at[m],
            head_s.at[m],
            head_r.at[m],
            group_peer(m),
        )
        for m in far_first(n_group)
    ]

    total = head_src[at16(chunk * first_group, chunk), :].astype(F32)
    for m, copy in zip(far_first(n_group), heads):
        copy.wait_recv()
        total = total + head_dst[m].astype(F32)
    col_src[:chunk, :] = total.astype(BF16)
    if piece * n_col > chunk:
        col_src[chunk:, :] = jnp.zeros((piece * n_col - chunk, LANES), BF16)
    cols = [
        push(col_src.at[at16(piece * col_of(m), piece), :], col_dst.at[m], col_s.at[m], col_r.at[m], col_peer(m))
        for m in far_first(n_col)
    ]

    for way in (1, -1):
        dirs[slot(way), :] = collect(way, (2 * way, 5 * way, 6 * way)).astype(BF16)
        give_back(way, way)

    own_piece = at16(piece * second_group, piece)
    total = col_src[own_piece, :].astype(F32)
    for m, copy in zip(far_first(n_col), cols):
        copy.wait_recv()
        total = total + col_dst[m].astype(F32)
    col_sum[own_piece, :] = total.astype(BF16)
    col_gathers = [
        push(col_sum.at[own_piece, :], col_sum.at[own_piece, :], cga_s.at[m], cga_r.at[m], col_peer(m))
        for m in far_first(n_col)
    ]

    for copy in lines + list(paired.values()) + heads:
        copy.wait_send()
    way = collect(0, (1, -1, 3, -3, 4, -4))
    unit = images[home, :].astype(F32)
    along = jnp.sum(unit * way, axis=1, keepdims=True)
    image_grad = ((way - unit * along) * image_inv).astype(BF16)
    for j in range(n_emb):
        back_src[j, :, :LANES] = image_grad[:, LANES * j : LANES * (j + 1)]
        back_src[j, :, LANES:] = image_grad[:, LANES * n_emb :]
    own_rows = at16(rows * k, rows)
    backs = [
        push(back_src.at[(k + m) % n_emb], back_dst.at[own_rows, :], back_s.at[m], back_r.at[m], emb_peer(m))
        for m in far_first(n_emb)
    ]
    back_dst[own_rows, :] = back_src[pl.ds(k, 1)][0]


    for copy in col_gathers:
        copy.wait_recv()
    own_chunk = at16(chunk * first_group, chunk)
    head_sum[own_chunk, :] = col_sum[:chunk, :]
    head_gathers = [
        push(col_sum.at[pl.ds(0, chunk), :], head_sum.at[own_chunk, :], hga_s.at[m], hga_r.at[m], group_peer(m))
        for m in far_first(n_group)
    ]

    for copy in backs:
        copy.wait_recv()
    turn_f[...] = jnp.transpose(back_dst[...].astype(F32))
    image_out[:LANES, :] = turn_f[:LANES, :].astype(BF16)
    image_out[LANES:, :] = turn_f[pl.ds(pl.multiple_of(LANES + tail * k, 16), tail), :].astype(BF16)

    for copy in list(returns.values()) + backs + cols + col_gathers:
        copy.wait_send()
    for copy in head_gathers:
        copy.wait_recv()
    for c in range(tiles):
        head_out[:, LANES * c : LANES * (c + 1)] = head_sum[depth * c : depth * (c + 1), :]

    for copy in head_gathers:
        copy.wait_send()


def on_device(image_emb, text_feat, head_weight, logit_scale, logit_bias):
    n_dp, n_emb = lax.axis_size("dp"), lax.axis_size("emb")
    depth, pairs = image_emb.shape
    width = text_feat.shape[0]
    rows = pairs // n_emb
    n_hi = n_emb // 2
    n_group, n_col = N_ZLO * N_X, N_Y
    slots = 2 * REACH + 1
    wide = LANES * n_emb + LANES
    chunk = up(depth * (width // LANES), 16 * n_group) // n_group
    piece = up(chunk, 16 * n_col) // n_col
    sizes = (n_dp, n_emb, depth, pairs, width, chunk, piece)
    scratch = [
        pltpu.VMEM((depth, pairs), BF16),
        pltpu.VMEM((width, pairs), BF16),
        pltpu.VMEM((depth, width), BF16),
        pltpu.VMEM((2 * LANES, pairs), F32),
        pltpu.VMEM((n_emb, rows + depth - LANES, LANES), BF16),
        pltpu.VMEM((n_emb, rows + depth - LANES, LANES), BF16),
        pltpu.VMEM((rows * slots, wide), BF16),
        pltpu.VMEM((depth * n_emb, pairs), BF16),
        pltpu.VMEM((wide, pairs), BF16),
        pltpu.VMEM((rows * slots, pairs), BF16),
        pltpu.VMEM((wide, pairs), F32),
        pltpu.VMEM((depth * n_emb, pairs), BF16),
        pltpu.VMEM((n_hi, depth, pairs), BF16),
        pltpu.VMEM((3, depth, pairs), BF16),
        pltpu.VMEM((3, depth, pairs), BF16),
        pltpu.VMEM((depth, pairs), BF16),
        pltpu.VMEM((rows * slots, wide), BF16),
        pltpu.VMEM((rows * slots, wide), BF16),
        pltpu.VMEM((n_emb, rows, 2 * LANES), BF16),
        pltpu.VMEM((pairs, 2 * LANES), BF16),
        pltpu.VMEM((chunk * n_group, LANES), BF16),
        pltpu.VMEM((n_group, chunk, LANES), BF16),
        pltpu.VMEM((piece * n_col, LANES), BF16),
        pltpu.VMEM((n_col, piece, LANES), BF16),
        pltpu.VMEM((piece * n_col, LANES), BF16),
        pltpu.VMEM((chunk * n_group, LANES), BF16),
    ]
    scratch.append(pltpu.SemaphoreType.DMA((3,)))
    for count in (n_emb, slots, 6, 4, n_hi, 4, 2, slots, n_emb, n_group, n_col, n_col, n_group):
        scratch += [pltpu.SemaphoreType.DMA((count,))] * 2
    hbm = pl.BlockSpec(memory_space=pltpu.HBM)
    smem = pl.BlockSpec(memory_space=pltpu.SMEM)
    vmem = pl.BlockSpec(memory_space=pltpu.VMEM)
    inputs = [
        pltpu.with_memory_space_constraint(x, pltpu.HBM)
        for x in (image_emb, text_feat, head_weight)
    ]
    image_grad, head_grad = pl.pallas_call(
        functools.partial(kernel, sizes),
        out_shape=(
            jax.ShapeDtypeStruct((depth, pairs), BF16),
            jax.ShapeDtypeStruct((depth, width), BF16),
        ),
        in_specs=[hbm, hbm, hbm, smem, smem],
        out_specs=(vmem, vmem),
        scratch_shapes=scratch,
        compiler_params=pltpu.CompilerParams(
            collective_id=0, has_side_effects=True, vmem_limit_bytes=40 * 1024 * 1024
        ),
    )(*inputs, logit_scale, logit_bias)
    return image_grad, head_grad.astype(F32)


def solution(mesh):
    placed = (P("emb", "dp"), P(None, "dp"), P("emb", None), P(), P())
    return jax.shard_map(
        on_device,
        mesh=mesh,
        in_specs=placed,
        out_specs=(P("emb", "dp"), P("emb", None)),
        check_vma=False,
    )
```

```python
import functools

import jax
import jax.numpy as jnp
from jax import lax
from jax.experimental import pallas as pl
from jax.experimental.pallas import tpu as pltpu
from jax.sharding import PartitionSpec as P

REACH = 6
EPSILON = 1e-06
N_ZLO, N_Y, N_X = 2, 8, 4
LANES = 128
ORDER = (0, 1, -1, 4, -4, 3, -3, 2, -2, 5, -5, 6, -6)
SLOT = {o: i for i, o in enumerate(ORDER)}
NEAR, MIDDLE = 7, 11
MESH = pl.DeviceIdType.MESH
BF16, F32 = jnp.bfloat16, jnp.float32


def up(value, step):
    return -(-value // step) * step


def kernel(
    sizes,
    image_hbm,
    feat_hbm,
    weight_hbm,
    scale_ref,
    bias_ref,
    image_out,
    head_out,
    image_ref,
    feat_ref,
    weight_ref,
    turn_f,
    swap_src,
    swap_dst,
    images,
    text_nat,
    text,
    weights,
    grad,
    text_part,
    pair_dst,
    line_src,
    line_dst,
    mid_dst,
    dirs,
    dirs_back,
    back_src,
    back_dst,
    head_src,
    head_dst,
    col_src,
    col_dst,
    col_sum,
    head_sum,
    load,
    swap_s,
    swap_r,
    win_s,
    win_r,
    gat_s,
    gat_r,
    fwd_s,
    fwd_r,
    pair_s,
    pair_r,
    line_s,
    line_r,
    mid_s,
    mid_r,
    ret_s,
    ret_r,
    back_s,
    back_r,
    head_s,
    head_r,
    col_s,
    col_r,
    cga_s,
    cga_r,
    hga_s,
    hga_r,
):
    n_dp, n_emb, depth, pairs, width, chunk, piece = sizes
    tail = depth - LANES
    rows = pairs // n_emb
    n_hi = n_emb // 2
    n_group, n_col = N_ZLO * N_X, N_Y
    wide = LANES * n_emb + LANES
    slots = 2 * REACH + 1
    me = lax.axis_index("dp")
    k = lax.axis_index("emb")
    hi, core = k // 2, k % 2
    x_at, y_at, z_at = me % N_X, (me // N_X) % N_Y, me // (N_X * N_Y)
    first_group = (z_at * N_X + x_at) * (1 - core) + y_at * core
    second_group = y_at * (1 - core) + (z_at * N_X + x_at) * core

    def emb_peer(m):
        return (me, (k + m) % n_emb)

    def dp_peer(offset):
        return ((me + offset + n_dp) % n_dp, k)

    partner = (me, k + 1 - 2 * core)

    def hi_of(m):
        return (hi + m) % n_hi

    def line_peer(m):
        return (me, 2 * hi_of(m) + core)

    def chip_at(plane, line):
        return (plane // N_X) * (N_X * N_Y) + line * N_X + plane % N_X

    plane_step = {4: 2, 3: 6, 5: 3, 2: 5, 6: 1, 1: 7, 7: 4}

    def group_of(m):
        return (first_group + plane_step[m] * (1 - core) + m * core) % n_group

    def group_peer(m):
        to = group_of(m)
        here, there = chip_at(to, y_at), chip_at(z_at * N_X + x_at, to)
        return (here * (1 - core) + there * core, k)

    def col_of(m):
        return (second_group + m * (1 - core) + plane_step[m] * core) % n_col

    def col_peer(m):
        to = col_of(m)
        here, there = chip_at(z_at * N_X + x_at, to), chip_at(to, y_at)
        return (here * (1 - core) + there * core, k)

    def at16(start, size):
        return pl.ds(pl.multiple_of(start, 16), size)

    def push(src, dst, send, recv, peer):
        copy = pltpu.make_async_remote_copy(
            src_ref=src,
            dst_ref=dst,
            send_sem=send,
            recv_sem=recv,
            device_id=peer,
            device_id_type=MESH,
        )
        copy.start()
        return copy

    def far_first(n):
        return sorted(range(1, n), key=lambda m: -min(m, n - m))

    def slot(o):
        return pl.ds(rows * SLOT[o], rows)

    def loaded(i, src, dst):
        copy = pltpu.make_async_copy(src, dst, load.at[i])
        copy.start()
        return copy

    loads = [
        loaded(0, image_hbm, image_ref),
        loaded(1, weight_hbm, weight_ref),
        loaded(2, feat_hbm, feat_ref),
    ]

    greeted = (
        [emb_peer(m) for m in far_first(n_emb)]
        + [dp_peer(o) for o in (1, -1, N_X, -N_X, N_X - 1, 1 - N_X, N_X + 1, -N_X - 1)]
        + [group_peer(m) for m in range(1, n_group)]
        + [col_peer(m) for m in range(1, n_col)]
    )
    barrier = pltpu.get_barrier_semaphore()
    for peer in greeted:
        pl.semaphore_signal(barrier, inc=1, device_id=peer, device_id_type=MESH)

    per = LANES // rows
    loads[0].wait()
    turned = jnp.transpose(image_ref[:LANES, :].astype(F32)).astype(BF16)
    for j in range(n_emb):
        swap_src[j, :rows, :] = turned[rows * j : rows * (j + 1)]
        at = LANES * (j // per)
        swap_src[j, rows:, :] = image_ref[LANES:, at : at + LANES]
    swap_dst[pl.ds(k, 1)] = swap_src[pl.ds(k, 1)]
    own_text = at16(depth * k, depth)
    loads[1].wait()
    loads[2].wait()
    text_nat[own_text, :] = jnp.dot(
        weight_ref[...], feat_ref[...], preferred_element_type=F32
    ).astype(BF16)

    pl.semaphore_wait(barrier, len(greeted))

    swaps = [
        push(
            swap_src.at[(k + m) % n_emb],
            swap_dst.at[k],
            swap_s.at[m],
            swap_r.at[m],
            emb_peer(m),
        )
        for m in far_first(n_emb)
    ]
    upper, lower = line_peer(1), line_peer(n_hi - 1)
    cut = up(depth // 2, 16)
    below_to = depth * (2 * ((hi + n_hi - 1) % n_hi) + core)
    above_to = depth * (2 * ((hi + 1) % n_hi) + core)

    def text_push(start, size, i, peer):
        at = at16(start, size)
        return push(text_nat.at[at, :], text_nat.at[at, :], gat_s.at[i], gat_r.at[i], peer)

    gathers = [
        text_push(depth * k, cut, 0, upper),
        text_push(depth * k + cut, depth - cut, 1, lower),
        text_push(depth * k + cut, depth - cut, 2, upper),
        text_push(depth * k, cut, 3, lower),
    ]
    forwards = [
        push(text_nat.at[own_text, :], text_nat.at[own_text, :], fwd_s.at[0], fwd_r.at[0], partner)
    ]

    for copy in swaps:
        copy.wait_recv()
    raw = [swap_dst[j, :rows, :].astype(F32) for j in range(n_emb)]
    tails = jnp.concatenate([swap_dst[j, rows:, :].astype(F32) for j in range(n_emb)], axis=0)
    turn_f[:LANES, :LANES] = jnp.transpose(tails)
    raw.append(turn_f[at16(rows * (k % per), rows), :LANES])
    square = sum(jnp.sum(r * r, axis=1, keepdims=True) for r in raw)
    image_inv = 1.0 / jnp.sqrt(square + EPSILON)
    home = slot(0)
    for j, r in enumerate(raw):
        images[home, LANES * j : LANES * (j + 1)] = (r * image_inv).astype(BF16)
    window = {}

    def pass_on(have, o):
        window[o] = push(
            images.at[slot(have), :],
            images.at[slot(o), :],
            win_s.at[SLOT[o]],
            win_r.at[SLOT[o]],
            dp_peer(have - o),
        )

    for o in (1, -1, N_X, -N_X, N_X - 1, 1 - N_X):
        pass_on(0, o)

    gathers[0].wait_recv()
    gathers.append(text_push(below_to, cut, 4, upper))
    gathers[1].wait_recv()
    gathers.append(text_push(above_to + cut, depth - cut, 5, lower))
    for i, need, come in ((1, 2, below_to), (2, 3, above_to)):
        gathers[need].wait_recv()
        come = at16(come, depth)
        forwards.append(
            push(text_nat.at[come, :], text_nat.at[come, :], fwd_s.at[i], fwd_r.at[i], partner)
        )

    for near in (1, -1):
        window[near].wait_recv()
        for o in (N_X + 2, N_X + 1, 2):
            pass_on(near, near * o)

    gathers[4].wait_recv()
    gathers[5].wait_recv()
    come = at16(depth * (2 * ((hi + 2) % n_hi) + core), depth)
    forwards.append(
        push(text_nat.at[come, :], text_nat.at[come, :], fwd_s.at[3], fwd_r.at[3], partner)
    )

    for copy in forwards:
        copy.wait_recv()
    if LANES > tail * n_emb:
        text[LANES * n_emb + tail * n_emb :, :] = jnp.zeros((LANES - tail * n_emb, pairs), BF16)
    square = jnp.zeros((1, pairs), F32)
    for j in range(n_emb):
        part = text_nat[depth * j : depth * (j + 1), :]
        text[LANES * j : LANES * (j + 1), :] = part[:LANES]
        text[LANES * n_emb + tail * j : LANES * n_emb + tail * (j + 1), :] = part[LANES:]
        wide_part = part.astype(F32)
        square = square + jnp.sum(wide_part * wide_part, axis=0, keepdims=True)
    text_inv = 1.0 / jnp.sqrt(square + EPSILON)

    scale, bias = scale_ref[0], bias_ref[0]

    def meet(first, last):
        at = pl.ds(rows * first, rows * (last - first))
        cosine = jnp.dot(images[at, :], text[...], preferred_element_type=F32) * text_inv
        logits = scale * cosine + bias
        if first == 0:
            row_ids = lax.broadcasted_iota(jnp.int32, logits.shape, 0)
            col_ids = lax.broadcasted_iota(jnp.int32, logits.shape, 1)
            same = (row_ids < rows) & (col_ids - rows * k == row_ids)
            sign = jnp.where(same, jnp.float32(1.0), jnp.float32(-1.0))
        else:
            sign = jnp.float32(-1.0)
        sig = 1.0 / (1.0 + jnp.exp(sign * logits))
        value = (-scale * sign * sig * text_inv).astype(BF16)
        weights[at, :] = value
        return jnp.sum(value.astype(F32) * cosine, axis=0, keepdims=True)

    def turn_back(first, last):
        at = pl.ds(rows * first, rows * (last - first))
        dirs[at, :] = lax.dot_general(
            weights[at, :], text[...], (((1,), (1,)), ((), ())), preferred_element_type=F32
        ).astype(BF16)

    def text_side(first, last):
        at = pl.ds(rows * first, rows * (last - first))
        return lax.dot_general(
            images[at, :], weights[at, :], (((0,), (0,)), ((), ())), preferred_element_type=F32
        )

    returns = {}

    def give_back(o, step):
        returns[o] = push(
            dirs.at[slot(o), :],
            dirs_back.at[slot(o), :],
            ret_s.at[SLOT[o]],
            ret_r.at[SLOT[o]],
            dp_peer(step),
        )

    def collect(o, sources):
        value = dirs[slot(o), :].astype(F32)
        for source in sources:
            returns[source].wait_recv()
            value = value + dirs_back[slot(source), :].astype(F32)
        return value

    for o in ORDER[3:NEAR]:
        window[o].wait_recv()
    inner = meet(0, NEAR)
    turn_back(0, NEAR)
    for way in (1, -1):
        give_back(4 * way, N_X * way)
        give_back(3 * way, (N_X - 1) * way)
    for o in ORDER[NEAR:MIDDLE]:
        window[o].wait_recv()
    inner = inner + meet(NEAR, MIDDLE)
    turn_back(NEAR, MIDDLE)
    for way in (1, -1):
        give_back(5 * way, N_X * way)
        give_back(2 * way, way)
    grad[...] = text_side(0, MIDDLE)
    for o in ORDER[MIDDLE:]:
        window[o].wait_recv()
    inner = (inner + meet(MIDDLE, len(ORDER))) * text_inv

    late = text_side(MIDDLE, len(ORDER))
    for j in range(n_emb):
        for at, size, to in ((LANES * j, LANES, 0), (LANES * n_emb + tail * j, tail, LANES)):
            part = grad[at : at + size, :] + late[at : at + size]
            part = part - text[at : at + size, :].astype(F32) * inner
            text_part[depth * j + to : depth * j + to + size, :] = part.astype(BF16)
    paired = {}
    for m in (2, 1, 3, 0):
        theirs = at16(depth * (2 * hi_of(m) + 1 - core), depth)
        paired[m] = push(text_part.at[theirs, :], pair_dst.at[m], pair_s.at[m], pair_r.at[m], partner)

    turn_back(MIDDLE, len(ORDER))
    for way in (1, -1):
        give_back(6 * way, (N_X + 1) * way)

    def summed(m):
        paired[m].wait_recv()
        mine = at16(depth * (2 * hi_of(m) + core), depth)
        return text_part[mine, :].astype(F32) + pair_dst[m].astype(F32)

    first, second = pl.ds(0, cut), pl.ds(cut, depth - cut)
    line_src[0] = summed(2).astype(BF16)
    lines = [
        push(line_src.at[0, first, :], mid_dst.at[first, :], mid_s.at[0], mid_r.at[0], upper),
        push(line_src.at[0, second, :], mid_dst.at[second, :], mid_s.at[1], mid_r.at[1], lower),
    ]
    rising, falling = summed(1), summed(3)
    line_src[1, cut:, :] = rising[cut:].astype(BF16)
    line_src[2, :cut, :] = falling[:cut].astype(BF16)

    def line(i, j, part, peer):
        return push(line_src.at[i, part, :], line_dst.at[i, part, :], line_s.at[j], line_r.at[j], peer)

    lines.append(line(1, 0, second, upper))
    lines.append(line(2, 1, first, lower))
    lines[0].wait_recv()
    line_src[1, :cut, :] = (rising[:cut] + mid_dst[:cut, :].astype(F32)).astype(BF16)
    lines.append(line(1, 2, first, upper))
    lines[1].wait_recv()
    line_src[2, cut:, :] = (falling[cut:] + mid_dst[cut:, :].astype(F32)).astype(BF16)
    lines.append(line(2, 3, second, lower))
    for copy in swaps + gathers + forwards + list(window.values()):
        copy.wait_send()
    total = summed(0)
    for copy in lines[2:]:
        copy.wait_recv()
    total = total + line_dst[1].astype(F32) + line_dst[2].astype(F32)

    share = lax.dot_general(
        total.astype(BF16), feat_ref[...], (((1,), (1,)), ((), ())), preferred_element_type=F32
    )
    tiles = width // LANES
    for c in range(tiles):
        head_src[depth * c : depth * (c + 1), :] = share[:, LANES * c : LANES * (c + 1)].astype(BF16)
    if chunk * n_group > depth * tiles:
        head_src[depth * tiles :, :] = jnp.zeros((chunk * n_group - depth * tiles, LANES), BF16)
    heads = [
        push(
            head_src.at[at16(chunk * group_of(m), chunk), :],
            head_dst.at[m],
            head_s.at[m],
            head_r.at[m],
            group_peer(m),
        )
        for m in far_first(n_group)
    ]

    total = head_src[at16(chunk * first_group, chunk), :].astype(F32)
    for m, copy in zip(far_first(n_group), heads):
        copy.wait_recv()
        total = total + head_dst[m].astype(F32)
    col_src[:chunk, :] = total.astype(BF16)
    if piece * n_col > chunk:
        col_src[chunk:, :] = jnp.zeros((piece * n_col - chunk, LANES), BF16)
    cols = [
        push(col_src.at[at16(piece * col_of(m), piece), :], col_dst.at[m], col_s.at[m], col_r.at[m], col_peer(m))
        for m in far_first(n_col)
    ]

    for way in (1, -1):
        dirs[slot(way), :] = collect(way, (2 * way, 5 * way, 6 * way)).astype(BF16)
        give_back(way, way)

    own_piece = at16(piece * second_group, piece)
    total = col_src[own_piece, :].astype(F32)
    for m, copy in zip(far_first(n_col), cols):
        copy.wait_recv()
        total = total + col_dst[m].astype(F32)
    col_sum[own_piece, :] = total.astype(BF16)
    col_gathers = [
        push(col_sum.at[own_piece, :], col_sum.at[own_piece, :], cga_s.at[m], cga_r.at[m], col_peer(m))
        for m in far_first(n_col)
    ]

    for copy in lines + list(paired.values()) + heads:
        copy.wait_send()
    way = collect(0, (1, -1, 3, -3, 4, -4))
    unit = images[home, :].astype(F32)
    along = jnp.sum(unit * way, axis=1, keepdims=True)
    image_grad = ((way - unit * along) * image_inv).astype(BF16)
    for j in range(n_emb):
        back_src[j, :, :LANES] = image_grad[:, LANES * j : LANES * (j + 1)]
        back_src[j, :, LANES:] = image_grad[:, LANES * n_emb :]
    own_rows = at16(rows * k, rows)
    backs = [
        push(back_src.at[(k + m) % n_emb], back_dst.at[own_rows, :], back_s.at[m], back_r.at[m], emb_peer(m))
        for m in far_first(n_emb)
    ]
    back_dst[own_rows, :] = back_src[pl.ds(k, 1)][0]


    for copy in col_gathers:
        copy.wait_recv()
    own_chunk = at16(chunk * first_group, chunk)
    head_sum[own_chunk, :] = col_sum[:chunk, :]
    head_gathers = [
        push(col_sum.at[pl.ds(0, chunk), :], head_sum.at[own_chunk, :], hga_s.at[m], hga_r.at[m], group_peer(m))
        for m in far_first(n_group)
    ]

    for copy in backs:
        copy.wait_recv()
    turn_f[...] = jnp.transpose(back_dst[...].astype(F32))
    image_out[:LANES, :] = turn_f[:LANES, :].astype(BF16)
    image_out[LANES:, :] = turn_f[pl.ds(pl.multiple_of(LANES + tail * k, 16), tail), :].astype(BF16)

    for copy in list(returns.values()) + backs + cols + col_gathers:
        copy.wait_send()
    for copy in head_gathers:
        copy.wait_recv()
    for c in range(tiles):
        head_out[:, LANES * c : LANES * (c + 1)] = head_sum[depth * c : depth * (c + 1), :]

    for copy in head_gathers:
        copy.wait_send()


def on_device(image_emb, text_feat, head_weight, logit_scale, logit_bias):
    n_dp, n_emb = lax.axis_size("dp"), lax.axis_size("emb")
    depth, pairs = image_emb.shape
    width = text_feat.shape[0]
    rows = pairs // n_emb
    n_hi = n_emb // 2
    n_group, n_col = N_ZLO * N_X, N_Y
    slots = 2 * REACH + 1
    wide = LANES * n_emb + LANES
    chunk = up(depth * (width // LANES), 16 * n_group) // n_group
    piece = up(chunk, 16 * n_col) // n_col
    sizes = (n_dp, n_emb, depth, pairs, width, chunk, piece)
    scratch = [
        pltpu.VMEM((depth, pairs), BF16),
        pltpu.VMEM((width, pairs), BF16),
        pltpu.VMEM((depth, width), BF16),
        pltpu.VMEM((2 * LANES, pairs), F32),
        pltpu.VMEM((n_emb, rows + depth - LANES, LANES), BF16),
        pltpu.VMEM((n_emb, rows + depth - LANES, LANES), BF16),
        pltpu.VMEM((rows * slots, wide), BF16),
        pltpu.VMEM((depth * n_emb, pairs), BF16),
        pltpu.VMEM((wide, pairs), BF16),
        pltpu.VMEM((rows * slots, pairs), BF16),
        pltpu.VMEM((wide, pairs), F32),
        pltpu.VMEM((depth * n_emb, pairs), BF16),
        pltpu.VMEM((n_hi, depth, pairs), BF16),
        pltpu.VMEM((3, depth, pairs), BF16),
        pltpu.VMEM((3, depth, pairs), BF16),
        pltpu.VMEM((depth, pairs), BF16),
        pltpu.VMEM((rows * slots, wide), BF16),
        pltpu.VMEM((rows * slots, wide), BF16),
        pltpu.VMEM((n_emb, rows, 2 * LANES), BF16),
        pltpu.VMEM((pairs, 2 * LANES), BF16),
        pltpu.VMEM((chunk * n_group, LANES), BF16),
        pltpu.VMEM((n_group, chunk, LANES), BF16),
        pltpu.VMEM((piece * n_col, LANES), BF16),
        pltpu.VMEM((n_col, piece, LANES), BF16),
        pltpu.VMEM((piece * n_col, LANES), BF16),
        pltpu.VMEM((chunk * n_group, LANES), BF16),
    ]
    scratch.append(pltpu.SemaphoreType.DMA((3,)))
    for count in (n_emb, slots, 6, 4, n_hi, 4, 2, slots, n_emb, n_group, n_col, n_col, n_group):
        scratch += [pltpu.SemaphoreType.DMA((count,))] * 2
    hbm = pl.BlockSpec(memory_space=pltpu.HBM)
    smem = pl.BlockSpec(memory_space=pltpu.SMEM)
    vmem = pl.BlockSpec(memory_space=pltpu.VMEM)
    inputs = [
        pltpu.with_memory_space_constraint(x, pltpu.HBM)
        for x in (image_emb, text_feat, head_weight)
    ]
    image_grad, head_grad = pl.pallas_call(
        functools.partial(kernel, sizes),
        out_shape=(
            jax.ShapeDtypeStruct((depth, pairs), BF16),
            jax.ShapeDtypeStruct((depth, width), BF16),
        ),
        in_specs=[hbm, hbm, hbm, smem, smem],
        out_specs=(vmem, vmem),
        scratch_shapes=scratch,
        compiler_params=pltpu.CompilerParams(
            collective_id=0, has_side_effects=True, vmem_limit_bytes=40 * 1024 * 1024
        ),
    )(*inputs, logit_scale, logit_bias)
    return image_grad, head_grad.astype(F32)


def solution(mesh):
    placed = (P("emb", "dp"), P(None, "dp"), P("emb", None), P(), P())
    return jax.shard_map(
        on_device,
        mesh=mesh,
        in_specs=placed,
        out_specs=(P("emb", "dp"), P("emb", None)),
        check_vma=False,
    )
```
